256 devices in a mesh: gx: 64 (over y_hi, z, x), gy: 4 (over y_lo, core).
Axes of the slice: x: 4, y: 4 (y_hi: 2, y_lo: 2; y = y_hi * 2 + y_lo), z: 8, core: 2. Of those that a mesh axis runs over, the one named last changes fastest.
Arguments:
- populations: float32 [19, 512, 64, 512], P(None, 'gx', 'gy'), as said below
- bead_frac: float32 [3, 1024, 512], P(None, 'gx', 'gy'), may hold values from 0 to 1
- bead_cell: int32 [1024, 512], P('gx', 'gy'), may hold values from 0 to 65535, as said below
- bead_charge: float32 [1024, 512], P('gx', 'gy'), may hold values from -3 to 3
- bead_velocity: float32 [3, 1024, 512], P(None, 'gx', 'gy'), may hold values from -1.5 to 1.5
- bead_count: int32 [1024, 4], P('gx', 'gy'), may hold values from 64 to 128
- pair_list: int32 [1024, 24], P('gx', 'gy'), may hold values from 0 to 47, as said below
Outputs:
- bead_force: float32 [3, 1024, 512], P(None, 'gx', 'gy')
- populations_next: float32 [19, 512, 64, 512], P(None, 'gx', 'gy')
The draws below stay inside these ranges and needn't reach their ends.
Inputs may be any that keep to these rules, and one draw needn't show every extreme that they name: `bead_cell`: the third part of a bead's cell lies in the third-dimension range of its block: c * 32 up to (c + 1) * 32 - 1, with c the block's row modulo 16; the first part is below 8, the second below 16. `pair_list`: the 6 codes of one block are distinct. Code k * 16 + e: for k = 0, e is c or c + 1 modulo 16; for k = 1 and k = 2, e is c - 1, c or c + 1 modulo 16; c is the block's row modulo 16. `populations`: each entry is 18 w_q (1 + t) with w_q the velocity's lattice weight and |t| at most 0.25.
All inputs are finite; a program needn't handle non-finite values.
Results may differ from the reference program's by a relative error of at most 0.0003.
Values sent between devices are 32-bit elements; how exact they have to be, the bound alone decides.
No kernel may reach another device: no remote copies, remote signals or barrier semaphores. Data moves between devices by JAX's collectives and lax.ppermute only.
A program may use at most 128 MiB of HBM per device.

```python
import jax
import jax.numpy as jnp
import numpy as np
from jax import lax

Q = 19
PLANES = 8
ROWS_Y = 16
LZ = 512
BLOCKS = 16
LANES = 128
SHELL = 6
NX = 512
NY = 64
BEAD_ROWS = 1024
BEAD_COLS = 512
N_GX = 64
N_GY = 4


LATTICE_WEIGHTS = np.array([1.0 / 3.0] + [1.0 / 18.0] * 6 + [1.0 / 36.0] * 12, np.float32)


LATTICE_VELOCITIES = np.array([[0, 0, 0], [1, 0, 0], [-1, 0, 0], [0, 1, 0], [0, -1, 0], [0, 0, 1], [0, 0, -1], [1, 1, 0], [-1, -1, 0], [1, -1, 0], [-1, 1, 0], [1, 0, 1], [-1, 0, -1], [1, 0, -1], [-1, 0, 1], [0, 1, 1], [0, -1, -1], [0, 1, -1], [0, -1, 1]], np.float32)


VELOCITY_SPANS = np.maximum(np.sum(np.abs(LATTICE_VELOCITIES), axis=1), 1.0).astype(np.float32)


WAVE_FIRST = [1.0, 1.0, 2.0]


WAVE_SECOND = [1.0, 2.0, 1.0]


WAVE_THIRD = [2.0, 1.0, 1.0]


SHELL_KINDS = [0, 0, 1, 1, 1, 2, 2, 2]


SHELL_STEPS = [0, 1, -1, 0, 1, -1, 0, 1]


def draw_populations(key, part):
    key = jax.random.fold_in(key, 3)
    key_spread, key_phase = jax.random.split(key)
    spread = jax.random.uniform(key_spread, (Q, NX, NY, LZ), jnp.float32, -1.0, 1.0)
    phases = jax.random.uniform(key_phase, (3,), jnp.float32, 0.0, 2.0 * np.pi)
    grid = (NX, NY, LZ)
    first = lax.broadcasted_iota(jnp.float32, grid, 0) / NX
    second = lax.broadcasted_iota(jnp.float32, grid, 1) / NY
    third = lax.broadcasted_iota(jnp.float32, grid, 2) / LZ
    coherent = jnp.zeros((Q, NX, NY, LZ), jnp.float32)
    for component in range(3):
        field = jnp.sin(2.0 * np.pi * (WAVE_FIRST[component] * first + WAVE_SECOND[component] * second + WAVE_THIRD[component] * third) + phases[component])
        factors = jnp.asarray(LATTICE_VELOCITIES[:, component] / VELOCITY_SPANS)
        coherent = coherent + factors[:, None, None, None] * field[None]
    lattice_weights = jnp.asarray(LATTICE_WEIGHTS)
    return 18.0 * lattice_weights[:, None, None, None] * (1.0 + 0.05 * spread + 0.2 * coherent)


def draw_bead_cell(key, part):
    key = jax.random.fold_in(key, 5)
    key_first, key_second, key_third = jax.random.split(key, 3)
    shape = (BEAD_ROWS, BEAD_COLS)
    first = jax.random.randint(key_first, shape, 0, PLANES)
    second = jax.random.randint(key_second, shape, 0, ROWS_Y)
    block_span = LZ // BLOCKS
    block_index = lax.broadcasted_iota(jnp.int32, shape, 0) % BLOCKS
    third = block_index * block_span + jax.random.randint(key_third, shape, 0, block_span)
    return ((first * ROWS_Y + second) * LZ + third).astype(jnp.int32)


def draw_pair_list(key, part):
    key = jax.random.fold_in(key, 9)
    columns = BEAD_COLS // LANES
    keys = jax.random.split(key, BEAD_ROWS * columns)
    picks = jax.vmap(lambda single: jax.random.permutation(single, 8))(keys)[:, :SHELL]
    picks = picks.reshape(BEAD_ROWS, columns, SHELL)
    kinds = jnp.asarray(SHELL_KINDS, jnp.int32)[picks]
    steps = jnp.asarray(SHELL_STEPS, jnp.int32)[picks]
    block_index = lax.broadcasted_iota(jnp.int32, (BEAD_ROWS, columns, SHELL), 0) % BLOCKS
    codes = kinds * BLOCKS + (block_index + steps + BLOCKS) % BLOCKS
    return codes.reshape(BEAD_ROWS, columns * SHELL).astype(jnp.int32)


def place_ends(entries, own_key, least, top_value):
    index_at = [jax.random.randint(jax.random.fold_in(own_key, axis), (), 0, length) for axis, length in enumerate(entries.shape)]
    widest = entries.shape.index(max(entries.shape))
    neighbour = index_at[:widest] + [(index_at[widest] + 1) % entries.shape[widest]] + index_at[widest + 1:]
    return entries.at[tuple(index_at)].set(least).at[tuple(neighbour)].set(top_value)


def block_scale(key, dims, cuts, low, top_value):
    def one(position, shards_of):
        heights = jax.random.uniform(jax.random.fold_in(jax.random.fold_in(key, 6), position), (shards_of,), jnp.float32, low / len(cuts), top_value / len(cuts))
        return jnp.repeat(jnp.exp(heights), dims[position] // shards_of).reshape((-1,) + (1,) * (len(dims) - position - 1))

    gain = one(*cuts[0])
    for cut in cuts[1:]:
        gain = gain * one(*cut)
    return gain


def bell_draw(stream_key, extent, width, reach, cuts=(), kind=jnp.bfloat16):
    entries = width * jax.random.normal(stream_key, extent, jnp.float32)
    if cuts:
        entries = entries * block_scale(stream_key, extent, cuts, -0.22, 0.18)
    return jnp.clip(entries, -reach, reach).astype(kind)


def setup_inputs(seed: int = 0) -> dict:
    key_list = jax.random.split(jax.random.key(seed), 8)
    populations = draw_populations(jax.random.fold_in(key_list[7], 71), 0)
    bead_frac = jnp.clip(1.0 * jax.random.uniform(key_list[1], (3, BEAD_ROWS, BEAD_COLS), jnp.float32) ** block_scale(key_list[1], (3, BEAD_ROWS, BEAD_COLS), ((1, 64), (2, 4)), -0.2, 0.2), 0.0, 1.0)
    bead_cell = draw_bead_cell(jax.random.fold_in(key_list[7], 71), 0)
    bead_charge = bell_draw(key_list[3], (BEAD_ROWS, BEAD_COLS), 1.0, 3.0, ((0, 64), (1, 4)), jnp.float32)
    bead_velocity = bell_draw(key_list[4], (3, BEAD_ROWS, BEAD_COLS), 0.1, 1.5, ((1, 64), (2, 4)), jnp.float32)
    bead_count = place_ends(jax.random.randint(key_list[5], (BEAD_ROWS, N_GY), LANES // 2, LANES + 1), jax.random.fold_in(key_list[5], 1), LANES // 2, LANES).astype(jnp.int32)
    pair_list = draw_pair_list(jax.random.fold_in(key_list[7], 71), 0)
    return dict(populations=populations, bead_frac=bead_frac, bead_cell=bead_cell, bead_charge=bead_charge, bead_velocity=bead_velocity, bead_count=bead_count, pair_list=pair_list)


VELOCITIES = np.array([[0, 0, 0], [1, 0, 0], [-1, 0, 0], [0, 1, 0], [0, -1, 0], [0, 0, 1], [0, 0, -1], [1, 1, 0], [-1, -1, 0], [1, -1, 0], [-1, 1, 0], [1, 0, 1], [-1, 0, -1], [1, 0, -1], [-1, 0, 1], [0, 1, 1], [0, -1, -1], [0, 1, -1], [0, -1, 1]], np.float32)
WEIGHTS = np.array([1.0 / 3.0] + [1.0 / 18.0] * 6 + [1.0 / 36.0] * 12, np.float32)
relaxation = 0.8
friction_rate = 8.0
screening = 0.25
softening = 0.25
gauss_term = 0.28209479177387814
coupling = 1.0

def block_forces(own_positions, own_charges, partner_positions, partner_charges, same_block, period_box):
    separation = own_positions[:, None, :, None] - partner_positions[:, :, None, :]
    period = period_box[:, None, None, None]
    separation = separation - period * jnp.floor(separation / period + 0.5)
    distance_sq = lax.optimization_barrier(jnp.sum(separation * separation, axis=0)) + softening
    distance = jnp.sqrt(distance_sq)
    radial = (lax.erfc(screening * distance) / distance + gauss_term * jnp.exp(-screening * screening * distance_sq)) / distance_sq
    lane_count = own_charges.shape[0]
    diagonal = lax.broadcasted_iota(jnp.int32, (lane_count, lane_count), 0) == lax.broadcasted_iota(jnp.int32, (lane_count, lane_count), 1)
    excluded = jnp.logical_and(same_block[:, None, None], diagonal[None])
    strength = coupling * own_charges[None, :, None] * partner_charges[:, None, :] * radial
    strength = jnp.where(excluded, jnp.zeros_like(strength), strength)
    vectors = strength[None] * separation
    return (lax.optimization_barrier(jnp.sum(vectors, axis=(1, 3))), -lax.optimization_barrier(jnp.sum(vectors, axis=2)))

def moments(populations):
    table = jnp.asarray(VELOCITIES, populations.dtype)
    density = lax.optimization_barrier(jnp.sum(populations, axis=0))
    momentum = jnp.einsum('qd,qxyz->dxyz', table, populations, precision=lax.Precision.HIGHEST)
    return (density, momentum)

def collide(populations, density, momentum, force_field):
    table = jnp.asarray(VELOCITIES, populations.dtype)
    lattice_weights = jnp.asarray(WEIGHTS, populations.dtype)
    velocity = (momentum + relaxation * force_field) / density[None]
    projected = jnp.einsum('qd,dxyz->qxyz', table, velocity, precision=lax.Precision.HIGHEST)
    speed_sq = lax.optimization_barrier(jnp.sum(velocity * velocity, axis=0))
    equilibrium = lattice_weights[:, None, None, None] * density[None] * (1.0 + 3.0 * projected + 4.5 * projected * projected - 1.5 * speed_sq[None])
    return populations - (populations - equilibrium) / relaxation

def corner_factor(fraction, offset):
    if offset == 1:
        return fraction
    return 1.0 - fraction

def split_beads(values):
    leading = values.shape[:-2]
    lead_count = len(leading)
    shaped = values.reshape(leading + (N_GX, BLOCKS, N_GY, LANES))
    axis_order = (lead_count, lead_count + 2) + tuple(range(lead_count)) + (lead_count + 1, lead_count + 3)
    return jnp.transpose(shaped, axis_order)

def reference(populations, bead_frac, bead_cell, bead_charge, bead_velocity, bead_count, pair_list):
    ftype = populations.dtype
    fraction = split_beads(bead_frac)
    cells = split_beads(bead_cell)
    charges = split_beads(bead_charge)
    velocity = split_beads(bead_velocity)
    counts = jnp.transpose(bead_count.reshape(N_GX, BLOCKS, N_GY), (0, 2, 1))
    live = (jnp.arange(LANES, dtype=jnp.int32)[None, None, None, :] < counts[..., None]).astype(ftype)
    slab_first = jnp.arange(N_GX, dtype=jnp.int32)[:, None, None, None]
    slab_second = jnp.arange(N_GY, dtype=jnp.int32)[None, :, None, None]
    base_first = slab_first * PLANES + cells // (ROWS_Y * LZ)
    base_second = slab_second * ROWS_Y + cells // LZ % ROWS_Y
    base_third = cells % LZ
    positions = jnp.stack([base_first.astype(ftype), base_second.astype(ftype), base_third.astype(ftype)], axis=2) + fraction
    charged = charges * live
    density, momentum = moments(populations)
    flow = momentum / density[None]
    fluid = jnp.zeros_like(positions)
    corners = []
    for offset_first in (0, 1):
        for offset_second in (0, 1):
            for offset_third in (0, 1):
                index_first = (base_first + offset_first) % NX
                index_second = (base_second + offset_second) % NY
                index_third = (base_third + offset_third) % LZ
                weight = corner_factor(fraction[:, :, 0], offset_first) * corner_factor(fraction[:, :, 1], offset_second) * corner_factor(fraction[:, :, 2], offset_third)
                fluid = fluid + weight[:, :, None] * jnp.moveaxis(flow[:, index_first, index_second, index_third], 0, 2)
                corners.append((index_first, index_second, index_third, weight))
    drag = friction_rate * (fluid - velocity) * live[:, :, None]
    force_field = jnp.zeros((3, NX, NY, LZ), ftype)
    for index_first, index_second, index_third, weight in corners:
        force_field = force_field.at[:, index_first, index_second, index_third].add(jnp.moveaxis(-drag * weight[:, :, None], 2, 0))
    period_box = jnp.array([NX, NY, LZ], ftype)
    candidates = jnp.concatenate([positions, jnp.roll(positions, -1, axis=0), jnp.roll(positions, -1, axis=1)], axis=3)
    candidate_charges = jnp.concatenate([charged, jnp.roll(charged, -1, axis=0), jnp.roll(charged, -1, axis=1)], axis=2)
    codes = jnp.transpose(pair_list.reshape(N_GX, BLOCKS, N_GY, SHELL), (0, 2, 1, 3))

    def one_device(entry):
        own_positions, own_charges, cand_positions, cand_charges, device_codes = entry
        partner_positions = cand_positions[:, device_codes]
        partner_charges = cand_charges[device_codes]
        same_block = device_codes == jnp.arange(BLOCKS, dtype=jnp.int32)[:, None]
        own_force, reaction = jax.vmap(block_forces, in_axes=(1, 0, 1, 0, 0, None), out_axes=(1, 1))(own_positions, own_charges, partner_positions, partner_charges, same_block, period_box)
        totals = jnp.zeros((3, 3 * BLOCKS, LANES), ftype).at[:, device_codes.reshape(-1)].add(reaction.reshape(3, BLOCKS * SHELL, LANES))
        return (own_force, totals)

    def per_device(values):
        return values.reshape((N_GX * N_GY,) + values.shape[2:])
    own_force, totals = lax.map(one_device, (per_device(positions), per_device(charged), per_device(candidates), per_device(candidate_charges), per_device(codes)))
    own_force = own_force.reshape(N_GX, N_GY, 3, BLOCKS, LANES)
    totals = totals.reshape(N_GX, N_GY, 3, 3 * BLOCKS, LANES)
    pair_force = own_force + totals[:, :, :, :BLOCKS] + jnp.roll(totals[:, :, :, BLOCKS:2 * BLOCKS], 1, axis=0) + jnp.roll(totals[:, :, :, 2 * BLOCKS:], 1, axis=1)
    combined = pair_force + drag
    bead_force = jnp.transpose(combined, (2, 0, 3, 1, 4)).reshape(3, N_GX * BLOCKS, N_GY * LANES)
    relaxed = collide(populations, density, momentum, force_field)
    passed = jnp.stack([jnp.roll(relaxed[velocity_index], shift=(int(VELOCITIES[velocity_index, 0]), int(VELOCITIES[velocity_index, 1]), int(VELOCITIES[velocity_index, 2])), axis=(0, 1, 2)) for velocity_index in range(Q)], axis=0)
    return (bead_force, passed)
```

```python
import functools

import jax
import jax.numpy as jnp
import numpy as np
from jax import lax
from jax.experimental import pallas as pl
from jax.experimental.pallas import tpu as pltpu
from jax.sharding import PartitionSpec as P

VELOCITIES = (
    (0, 0, 0),
    (1, 0, 0),
    (-1, 0, 0),
    (0, 1, 0),
    (0, -1, 0),
    (0, 0, 1),
    (0, 0, -1),
    (1, 1, 0),
    (-1, -1, 0),
    (1, -1, 0),
    (-1, 1, 0),
    (1, 0, 1),
    (-1, 0, -1),
    (1, 0, -1),
    (-1, 0, 1),
    (0, 1, 1),
    (0, -1, -1),
    (0, 1, -1),
    (0, -1, 1),
)
Q = 19
FACE = 1.0 / 18.0
EDGE = 1.0 / 36.0
relaxation = 0.8
friction_rate = 8.0
screening = 0.25
softening = 0.25
gauss_term = 0.28209479177387814

STRETCH = 0.45
ERFCX = (
    0.2538730335007913,
    0.2542496247938967,
    0.22382455836296578,
    0.20419679225971624,
    0.007848770232788184,
    0.247605942768305,
    -0.264920441150418,
    0.07332591039690019,
)

PLANES = 8
ROWS = 16
LENGTH = 512
BLOCKS = 16
LANES = 128
SHELL = 6
SPAN = LENGTH // BLOCKS
NODES = PLANES * ROWS
WINDOW = 160

X_UP = tuple(q for q in range(Q) if VELOCITIES[q][0] == 1)
X_DOWN = tuple(q for q in range(Q) if VELOCITIES[q][0] == -1)
Y_UP = tuple(q for q in range(Q) if VELOCITIES[q][1] == 1)
Y_DOWN = tuple(q for q in range(Q) if VELOCITIES[q][1] == -1)
HIGHEST = lax.Precision.HIGHEST
VMEM = pltpu.VMEM
WHOLE = pl.BlockSpec(memory_space=pltpu.VMEM)
SCALARS = pl.BlockSpec(memory_space=pltpu.SMEM)
UNREAD = pl.BlockSpec(memory_space=pl.ANY)


def params(mib):
    return pltpu.CompilerParams(vmem_limit_bytes=mib * 1024 * 1024)


def f32(*shape):
    return jax.ShapeDtypeStruct(shape, jnp.float32)


def pack_kernel(base_ref, cell_ref, frac_ref, charge_ref, velocity_ref, count_ref, pair_ref, drag_ref):
    cell = cell_ref[...]
    first = lax.shift_right_logical(cell, 13)
    second = lax.shift_right_logical(cell, 9) & 15
    third = cell & 511
    block = lax.broadcasted_iota(jnp.int32, (BLOCKS, LANES), 0)
    lane = lax.broadcasted_iota(jnp.int32, (BLOCKS, LANES), 1)
    start_first = base_ref[0]
    start_second = base_ref[1]
    start_third = block * SPAN
    x = (start_first + first).astype(jnp.float32) + frac_ref[0]
    y = (start_second + second).astype(jnp.float32) + frac_ref[1]
    z = third.astype(jnp.float32) + frac_ref[2]
    x = x - start_first.astype(jnp.float32)
    y = y - start_second.astype(jnp.float32)
    z = z - start_third.astype(jnp.float32)
    live = (lane < count_ref[...]).astype(jnp.float32)
    charged = charge_ref[...] * live
    pairs = (x, y, z, charged)
    drags = (
        first.astype(jnp.float32),
        second.astype(jnp.float32),
        (third - start_third).astype(jnp.float32),
        frac_ref[0],
        frac_ref[1],
        frac_ref[2],
        velocity_ref[0],
        velocity_ref[1],
        velocity_ref[2],
        live,
    )
    zeros = jnp.zeros((8, LANES), jnp.float32)
    for c in range(BLOCKS):
        pair_ref[c, :, :] = zeros
        drag_ref[c, 8:16, :] = zeros
        for k, value in enumerate(pairs):
            pair_ref[c, k : k + 1, :] = value[c : c + 1]
        for k, value in enumerate(drags):
            drag_ref[c, k : k + 1, :] = value[c : c + 1]


def pack(base, cell, frac, charge, velocity, count):
    return pl.pallas_call(
        pack_kernel,
        out_shape=(f32(BLOCKS, 8, LANES), f32(BLOCKS, 16, LANES)),
        in_specs=[SCALARS] + [WHOLE] * 5,
        out_specs=(WHOLE, WHOLE),
        compiler_params=params(16),
        name="pack",
    )(base, cell, frac, charge, velocity, count)


def moments_of(pops):
    rho = pops[0]
    for q in range(1, Q):
        rho = rho + pops[q]
    momentum = []
    for d in range(3):
        total = None
        for q in range(Q):
            sign = VELOCITIES[q][d]
            if sign == 0:
                continue
            if total is None:
                total = pops[q]
            elif sign > 0:
                total = total + pops[q]
            else:
                total = total - pops[q]
        momentum.append(total)
    return rho, momentum


def flow_kernel(pop_ref, flow_ref, plane_ref, row_ref, corner_ref):
    p = pl.program_id(0)
    rho, momentum = moments_of([pop_ref[q, 0] for q in range(Q)])
    inverse = 1.0 / rho
    flow = [m * inverse for m in momentum]
    for d in range(3):
        flow_ref[d] = flow[d]
        row_ref[d, pl.ds(p, 1), :] = flow[d][0:1]

    @pl.when(p == 0)
    def _():
        for d in range(3):
            plane_ref[d] = flow[d]
            corner_ref[d : d + 1, :] = flow[d][0:1]


def flow_of(populations):
    return pl.pallas_call(
        flow_kernel,
        grid=(PLANES,),
        out_shape=(
            f32(3, NODES, LENGTH),
            f32(3, ROWS, LENGTH),
            f32(3, PLANES, LENGTH),
            f32(8, LENGTH),
        ),
        in_specs=[pl.BlockSpec((Q, 1, ROWS, LENGTH), lambda p: (0, p, 0, 0))],
        out_specs=(
            pl.BlockSpec((3, ROWS, LENGTH), lambda p: (0, p, 0)),
            pl.BlockSpec((3, ROWS, LENGTH), lambda p: (0, 0, 0)),
            pl.BlockSpec((3, PLANES, LENGTH), lambda p: (0, 0, 0)),
            pl.BlockSpec((8, LENGTH), lambda p: (0, 0)),
        ),
        compiler_params=params(32),
        cost_estimate=pl.CostEstimate(flops=4000000, bytes_accessed=6000000, transcendentals=0),
        name="flow",
    )(populations)


def radial_of(s):
    r = lax.rsqrt(s)
    rr = s * r
    t = 1.0 / (1.0 + (STRETCH * screening) * rr)
    poly = jnp.full_like(t, ERFCX[-1])
    for coefficient in ERFCX[-2::-1]:
        poly = poly * t + coefficient
    return jnp.exp(s * (-screening * screening)) * (poly * t * r + gauss_term) * (r * r)


def pair_tiles(kind, codes_ref, own_ref, cand_ref, own_out, react_out, wide, acc):
    shift_first = 8.0 if kind == 1 else 0.0
    shift_second = 16.0 if kind == 2 else 0.0
    react_out[...] = jnp.zeros_like(react_out)
    ones = jnp.ones((8, LANES), jnp.float32)

    def block(c, carry):
        columns = own_ref[c].T
        for k in range(4):
            wide[k] = jnp.broadcast_to(columns[:, k : k + 1], (LANES, LANES))
        acc[...] = jnp.zeros_like(acc)
        for s in range(SHELL):
            code = codes_ref[c, s]

            @pl.when(lax.shift_right_logical(code, 4) == kind)
            def _():
                e = code & 15
                steps = e - c
                steps = jnp.where(steps > 1, steps - BLOCKS, steps)
                steps = jnp.where(steps < -1, steps + BLOCKS, steps)
                shift_third = (steps * SPAN).astype(jnp.float32)
                cand = cand_ref[e]
                xj = jnp.broadcast_to(cand[0:1] + shift_first, (8, LANES))
                yj = jnp.broadcast_to(cand[1:2] + shift_second, (8, LANES))
                zj = jnp.broadcast_to(cand[2:3] + shift_third, (8, LANES))
                qj = jnp.broadcast_to(cand[3:4], (8, LANES))
                sums = [jnp.zeros((8, LANES), jnp.float32) for _ in range(3)]
                for g in range(LANES // 8):
                    rows = slice(8 * g, 8 * g + 8)
                    dx = wide[0, rows] - xj
                    dy = wide[1, rows] - yj
                    dz = wide[2, rows] - zj
                    squares = dx * dx + dy * dy + dz * dz + softening
                    strength = wide[3, rows] * qj * radial_of(squares)
                    if kind == 0:
                        i = lax.broadcasted_iota(jnp.int32, (8, LANES), 0) + 8 * g
                        j = lax.broadcasted_iota(jnp.int32, (8, LANES), 1)
                        gap = jnp.abs(i - j) + jnp.abs(steps)
                        strength = jnp.where(gap == 0, 0.0, strength)
                    for d, delta in enumerate((dx, dy, dz)):
                        force = strength * delta
                        acc[d, rows] = acc[d, rows] + force
                        sums[d] = sums[d] + force
                for d in range(3):
                    total = jnp.sum(sums[d], axis=0, keepdims=True)
                    react_out[e, d : d + 1, :] = react_out[e, d : d + 1, :] - total

        rows = lax.dot_general(
            ones,
            acc[...].reshape(3 * LANES, LANES),
            (((1,), (1,)), ((), ())),
            precision=HIGHEST,
            preferred_element_type=jnp.float32,
        )
        for d in range(3):
            own_out[c, d : d + 1, :] = rows[0:1, d * LANES : (d + 1) * LANES]
        return carry

    lax.fori_loop(0, BLOCKS, block, 0)


def pair_kernel(kind, codes_ref, own_ref, cand_ref, after_ref, own_out, react_out, wide, acc):
    del after_ref
    own_out[...] = jnp.zeros_like(own_out)
    pair_tiles(kind, codes_ref, own_ref, cand_ref, own_out, react_out, wide, acc)


def pair_last_kernel(
    codes_ref,
    own_ref,
    cand_ref,
    after_ref,
    own_1,
    own_2,
    back_1,
    back_2,
    drag_ref,
    out_ref,
    own_out,
    react_out,
    wide,
    acc,
):
    del after_ref
    own_out[...] = jnp.zeros_like(own_out)
    pair_tiles(0, codes_ref, own_ref, cand_ref, own_out, react_out, wide, acc)
    for c in range(BLOCKS):
        total = own_out[c] + react_out[c] + own_1[c] + own_2[c] + back_1[c] + back_2[c] + drag_ref[c]
        for d in range(3):
            out_ref[d, c : c + 1, :] = total[d : d + 1]


PAIR_COST = pl.CostEstimate(flops=60000000, bytes_accessed=1000000, transcendentals=1500000)
PAIR_SCRATCH = [VMEM((4, LANES, LANES), jnp.float32), VMEM((3, LANES, LANES), jnp.float32)]


def pair(kind, codes, own, cand, after):
    return pl.pallas_call(
        functools.partial(pair_kernel, kind),
        out_shape=(f32(BLOCKS, 8, LANES), f32(BLOCKS, 8, LANES)),
        in_specs=[SCALARS, WHOLE, WHOLE, UNREAD],
        out_specs=(WHOLE, WHOLE),
        scratch_shapes=PAIR_SCRATCH,
        compiler_params=params(16),
        cost_estimate=PAIR_COST,
        name="pair_" + str(kind),
    )(codes, own, cand, after)


def pair_last(codes, own, cand, after, own_1, own_2, back_1, back_2, drag):
    return pl.pallas_call(
        pair_last_kernel,
        out_shape=f32(3, BLOCKS, LANES),
        in_specs=[SCALARS, WHOLE, WHOLE, UNREAD] + [WHOLE] * 5,
        out_specs=WHOLE,
        scratch_shapes=[VMEM((BLOCKS, 8, LANES), jnp.float32)] * 2 + PAIR_SCRATCH,
        compiler_params=params(16),
        cost_estimate=PAIR_COST,
        name="pair_0",
    )(codes, own, cand, after, own_1, own_2, back_1, back_2, drag)


def hat(steps, fraction):
    return jnp.where(steps == 0.0, 1.0 - fraction, jnp.where(steps == 1.0, fraction, 0.0))


def node_first(k):
    value = jnp.where(k < NODES, lax.shift_right_logical(k, 4), PLANES)
    value = jnp.where(k < NODES + ROWS, value, k - (NODES + ROWS))
    value = jnp.where(k < NODES + ROWS + PLANES, value, PLANES)
    return jnp.where(k < NODES + ROWS + PLANES + 1, value, -8).astype(jnp.float32)


def node_second(k):
    value = jnp.where(k < NODES + ROWS, k & 15, ROWS)
    return jnp.where(k < NODES + ROWS + PLANES + 1, value, -8).astype(jnp.float32)


def friction_kernel(
    bead_ref,
    flow_ref,
    plane_ref,
    row_ref,
    corner_ref,
    drag_ref,
    field_ref,
    ghost_plane_ref,
    ghost_row_ref,
    ghost_corner_ref,
    total_ref,
):
    width = SPAN + 1
    k_lane = lax.broadcasted_iota(jnp.int32, (1, WINDOW), 1)
    k_row = lax.broadcasted_iota(jnp.int32, (WINDOW, 1), 0)
    first_lane, second_lane = node_first(k_lane), node_second(k_lane)
    first_row, second_row = node_first(k_row), node_second(k_row)
    lane = lax.broadcasted_iota(jnp.int32, (1, LANES), 1)
    part = (lane >= width).astype(jnp.int32) + (lane >= 2 * width).astype(jnp.int32)
    part = jnp.where(lane < 3 * width, part, -1)
    depth = jnp.where(part >= 0, lane - part * width, -8).astype(jnp.float32)
    part_row = lax.broadcasted_iota(jnp.int32, (LANES, 1), 0)
    part_row = jnp.where(
        part_row < 3 * width,
        (part_row >= width).astype(jnp.int32) + (part_row >= 2 * width).astype(jnp.int32),
        -2,
    )
    spread_sum = (part_row == part).astype(jnp.float32)
    eight = lax.broadcasted_iota(jnp.int32, (8, 1), 0)
    pick = (eight == part).astype(jnp.float32)
    lane_full = lax.broadcasted_iota(jnp.int32, (WINDOW, LANES), 1)
    padding = jnp.zeros((WINDOW - NODES - ROWS - PLANES - 1, LANES), jnp.float32)
    total_ref[...] = jnp.zeros_like(total_ref)
    dot = functools.partial(jnp.dot, precision=HIGHEST, preferred_element_type=jnp.float32)

    for j in range(LENGTH // LANES):
        lanes = slice(j * LANES, (j + 1) * LANES)
        later = (j + 1) % (LENGTH // LANES)
        lanes_next = slice(later * LANES, (later + 1) * LANES)

        def window(d, cut):
            return jnp.concatenate(
                [
                    flow_ref[d, :, cut],
                    plane_ref[d, :, cut],
                    row_ref[d, :, cut],
                    corner_ref[d : d + 1, cut],
                    padding,
                ],
                axis=0,
            )

        here = [window(d, lanes) for d in range(3)]
        wrapped = [jnp.where(lane_full == 0, window(d, lanes_next), here[d]) for d in range(3)]
        sums = [jnp.zeros((WINDOW, LANES), jnp.float32) for _ in range(3)]
        for m in range(LANES // SPAN):
            c = j * (LANES // SPAN) + m
            source = here if m < 3 else wrapped
            turned = [
                pltpu.roll(source[d], (width * d - SPAN * m) % LANES, 1)
                if (width * d - SPAN * m) % LANES
                else source[d]
                for d in range(3)
            ]
            right = jnp.where(
                lane_full < width,
                turned[0],
                jnp.where(lane_full < 2 * width, turned[1], turned[2]),
            )
            rows = bead_ref[c]
            columns = rows.T
            column = [columns[:, k : k + 1] for k in range(10)]
            weight = hat(first_lane - column[0], column[3]) * hat(second_lane - column[1], column[4])
            weight_t = hat(first_row - rows[0:1], rows[3:4]) * hat(second_row - rows[1:2], rows[4:5])
            along = hat(depth - column[2], column[5])
            weighted = dot(weight, right) * along
            fluid = dot(weighted, spread_sum)
            speed = jnp.where(part == 0, column[6], jnp.where(part == 1, column[7], column[8]))
            push = (friction_rate * column[9]) * (speed - fluid) * along
            fluid_rows = lax.dot_general(
                pick,
                weighted,
                (((1,), (1,)), ((), ())),
                precision=HIGHEST,
                preferred_element_type=jnp.float32,
            )
            for d in range(3):
                drag_ref[c, d : d + 1, :] = (
                    friction_rate * (fluid_rows[d : d + 1] - rows[6 + d : 7 + d]) * rows[9:10]
                )
            drag_ref[c, 3:8, :] = jnp.zeros((5, LANES), jnp.float32)
            spread = dot(weight_t, push)
            for d in range(3):
                amount = (SPAN * m - width * d) % LANES
                back = pltpu.roll(spread, amount, 1) if amount else spread
                if m < 3:
                    inside = jnp.logical_and(lane_full >= SPAN * m, lane_full <= SPAN * (m + 1))
                    sums[d] = sums[d] + jnp.where(inside, back, 0.0)
                else:
                    sums[d] = sums[d] + jnp.where(lane_full >= SPAN * m, back, 0.0)
                    total_ref[d, :, lanes_next] = total_ref[d, :, lanes_next] + jnp.where(
                        lane_full == 0, back, 0.0
                    )
        for d in range(3):
            total_ref[d, :, lanes] = total_ref[d, :, lanes] + sums[d]
    ghost_corner_ref[...] = jnp.zeros_like(ghost_corner_ref)
    for d in range(3):
        field_ref[d] = total_ref[d, 0:NODES]
        ghost_plane_ref[d] = total_ref[d, NODES : NODES + ROWS]
        ghost_row_ref[d] = total_ref[d, NODES + ROWS : NODES + ROWS + PLANES]
        ghost_corner_ref[d : d + 1, :] = total_ref[d, NODES + ROWS + PLANES : NODES + ROWS + PLANES + 1]


def friction(beads, flow, plane, row, corner):
    return pl.pallas_call(
        friction_kernel,
        out_shape=(
            f32(BLOCKS, 8, LANES),
            f32(3, NODES, LENGTH),
            f32(3, ROWS, LENGTH),
            f32(3, PLANES, LENGTH),
            f32(8, LENGTH),
        ),
        in_specs=[WHOLE] * 5,
        out_specs=(WHOLE,) * 5,
        scratch_shapes=[VMEM((3, WINDOW, LENGTH), jnp.float32)],
        compiler_params=params(32),
        cost_estimate=pl.CostEstimate(flops=60000000, bytes_accessed=3000000, transcendentals=0),
        name="friction",
    )(beads, flow, plane, row, corner)


def collide_kernel(
    pop_hbm,
    field_ref,
    plane_ref,
    row_ref,
    corner_ref,
    out_hbm,
    x_up,
    x_down,
    y_up,
    y_down,
    corners,
    pop,
    out,
    in_sems,
    out_sems,
):
    def load(p):
        return pltpu.make_async_copy(pop_hbm.at[:, p], pop.at[:, p], in_sems.at[p])

    def store(p):
        return pltpu.make_async_copy(out.at[:, p], out_hbm.at[:, p], out_sems.at[p])

    for p in range(PLANES):
        load(p).start()
    row_index = lax.broadcasted_iota(jnp.int32, (ROWS, LENGTH), 0)
    for p in range(PLANES):
        load(p).wait()
        rho, momentum = moments_of([pop[q, p] for q in range(Q)])
        inverse = 1.0 / rho
        velocity = []
        for d in range(3):
            force = field_ref[d, p * ROWS : (p + 1) * ROWS]
            edge = row_ref[d, p : p + 1]
            if p == 0:
                force = force + plane_ref[d]
                edge = edge + corner_ref[d : d + 1]
            force = force + jnp.where(row_index == 0, edge, 0.0)
            velocity.append((momentum[d] + relaxation * force) * inverse)
        speed = velocity[0] * velocity[0] + velocity[1] * velocity[1] + velocity[2] * velocity[2]
        base = 1.0 - 1.5 * speed
        weights = (rho * (1.25 / 3.0), rho * (1.25 * FACE), rho * (1.25 * EDGE))
        for q in range(Q):
            cx, cy, cz = VELOCITIES[q]
            moving = abs(cx) + abs(cy) + abs(cz)
            equilibrium = base
            if moving:
                projected = None
                for sign, component in zip((cx, cy, cz), velocity):
                    if sign == 0:
                        continue
                    if projected is None:
                        projected = component if sign > 0 else -component
                    elif sign > 0:
                        projected = projected + component
                    else:
                        projected = projected - component
                equilibrium = base + projected * (3.0 + 4.5 * projected)
            relaxed = weights[moving] * equilibrium - 0.25 * pop[q, p]
            if cz:
                relaxed = pltpu.roll(relaxed, cz % LENGTH, 1)
            if cy:
                relaxed = pltpu.roll(relaxed, cy % ROWS, 0)
            target = (p + cx) % PLANES
            out[q, target] = relaxed
            if cy == 1:
                y_up[Y_UP.index(q), target : target + 1, :] = relaxed[0:1]
            if cy == -1:
                y_down[Y_DOWN.index(q), target : target + 1, :] = relaxed[ROWS - 1 : ROWS]
            if cx == 1 and target == 0:
                x_up[X_UP.index(q)] = relaxed
            if cx == -1 and target == PLANES - 1:
                x_down[X_DOWN.index(q)] = relaxed
            if 7 <= q <= 10 and target == (0 if cx == 1 else PLANES - 1):
                row = 0 if cy == 1 else ROWS - 1
                corners[q - 7, 0:1, :] = relaxed[row : row + 1]
        if 2 <= p:
            store(p - 1).start()
    store(0).start()
    store(PLANES - 1).start()
    for p in range(PLANES):
        store(p).wait()


def collide(populations, field, plane, row, corner):
    return pl.pallas_call(
        collide_kernel,
        out_shape=(
            f32(Q, PLANES, ROWS, LENGTH),
            f32(5, ROWS, LENGTH),
            f32(5, ROWS, LENGTH),
            f32(5, PLANES, LENGTH),
            f32(5, PLANES, LENGTH),
            f32(4, 8, LENGTH),
        ),
        in_specs=[UNREAD] + [WHOLE] * 4,
        out_specs=(UNREAD,) + (WHOLE,) * 5,
        scratch_shapes=[
            VMEM((Q, PLANES, ROWS, LENGTH), jnp.float32),
            VMEM((Q, PLANES, ROWS, LENGTH), jnp.float32),
            pltpu.SemaphoreType.DMA((PLANES,)),
            pltpu.SemaphoreType.DMA((PLANES,)),
        ],
        compiler_params=params(40),
        cost_estimate=pl.CostEstimate(flops=20000000, bytes_accessed=12000000, transcendentals=0),
        name="collide",
    )(populations, field, plane, row, corner)


def patch_kernel(
    out_in, x_up, x_down, y_up, y_down, c_7, c_8, c_9, c_10, out_hbm, tiles, faces, sems, face_sems
):
    del out_in
    sides = ((Y_UP, y_up, 0), (Y_DOWN, y_down, 8))
    for side, (group, unused, start) in enumerate(sides):
        for n, q in enumerate(group):
            pltpu.make_async_copy(
                out_hbm.at[q, :, pl.ds(start, 8)], tiles.at[side, n], sems.at[side, n]
            ).start()
    corner = {7: c_7, 8: c_8, 9: c_9, 10: c_10}
    ends = ((X_UP, x_up, 0), (X_DOWN, x_down, PLANES - 1))
    for end, (group, received, plane) in enumerate(ends):
        for n, q in enumerate(group):
            faces[end, n] = received[n]
            if VELOCITIES[q][1] == 1:
                faces[end, n, 0:1, :] = corner[q][0:1, :]
            if VELOCITIES[q][1] == -1:
                faces[end, n, ROWS - 1 : ROWS, :] = corner[q][0:1, :]
            if VELOCITIES[q][1] == 0:
                pltpu.make_async_copy(
                    faces.at[end, n], out_hbm.at[q, plane], face_sems.at[end, n]
                ).start()
    for side, (group, received, start) in enumerate(sides):
        row = 0 if side == 0 else 7
        for n, q in enumerate(group):
            pltpu.make_async_copy(
                out_hbm.at[q, :, pl.ds(start, 8)], tiles.at[side, n], sems.at[side, n]
            ).wait()
            for p in range(PLANES):
                tiles[side, n, p, row : row + 1, :] = received[n, p : p + 1, :]
            pltpu.make_async_copy(
                tiles.at[side, n], out_hbm.at[q, :, pl.ds(start, 8)], sems.at[side, n]
            ).start()
    for side, (group, unused, start) in enumerate(sides):
        for n, q in enumerate(group):
            pltpu.make_async_copy(
                tiles.at[side, n], out_hbm.at[q, :, pl.ds(start, 8)], sems.at[side, n]
            ).wait()
    for end, (group, unused, plane) in enumerate(ends):
        for n, q in enumerate(group):
            if VELOCITIES[q][1] != 0:
                pltpu.make_async_copy(
                    faces.at[end, n], out_hbm.at[q, plane], face_sems.at[end, n]
                ).start()
    for end, (group, unused, plane) in enumerate(ends):
        for n, q in enumerate(group):
            pltpu.make_async_copy(faces.at[end, n], out_hbm.at[q, plane], face_sems.at[end, n]).wait()


def patch(out, received):
    return pl.pallas_call(
        patch_kernel,
        out_shape=f32(Q, PLANES, ROWS, LENGTH),
        in_specs=[UNREAD] + [WHOLE] * 8,
        out_specs=UNREAD,
        scratch_shapes=[
            VMEM((2, 5, PLANES, 8, LENGTH), jnp.float32),
            VMEM((2, 5, ROWS, LENGTH), jnp.float32),
            pltpu.SemaphoreType.DMA((2, 5)),
            pltpu.SemaphoreType.DMA((2, 5)),
        ],
        input_output_aliases={0: 0},
        compiler_params=params(24),
        cost_estimate=pl.CostEstimate(flops=1000, bytes_accessed=4000000, transcendentals=0),
        name="patch",
    )(out, *received)


def on_device(n_first, n_second, populations, frac, cell, charge, velocity, count, codes):
    def to(value, steps_first, steps_second):
        pairs = [
            (
                i * n_second + j,
                ((i + steps_first) % n_first) * n_second + (j + steps_second) % n_second,
            )
            for i in range(n_first)
            for j in range(n_second)
        ]
        return lax.ppermute(value, ("gx", "gy"), pairs)

    base = jnp.stack([lax.axis_index("gx") * PLANES, lax.axis_index("gy") * ROWS]).astype(jnp.int32)
    pairs, beads = pack(base, cell, frac, charge, velocity, count)
    pairs_1 = to(pairs, -1, 0)
    pairs_2 = to(pairs, 0, -1)
    flow, plane, row, corner = flow_of(populations)
    plane, row, corner = to(plane, -1, 0), to(row, 0, -1), to(corner, -1, -1)
    own_1, react_1 = pair(1, codes, pairs, pairs_1, flow)
    drag, field, plane, row, corner = friction(beads, flow, plane, row, corner)
    back_1 = to(react_1, 1, 0)
    plane, row, corner = to(plane, 1, 0), to(row, 0, 1), to(corner, 1, 1)
    own_2, react_2 = pair(2, codes, pairs, pairs_2, drag)
    back_2 = to(react_2, 0, 1)
    out, x_up, x_down, y_up, y_down, corners = collide(populations, field, plane, row, corner)
    received = [to(x_up, 1, 0), to(x_down, -1, 0), to(y_up, 0, 1), to(y_down, 0, -1)]
    for q in range(7, 11):
        received.append(to(corners[q - 7], VELOCITIES[q][0], VELOCITIES[q][1]))
    force = pair_last(codes, pairs, pairs, out, own_1, own_2, back_1, back_2, drag)
    return force, patch(out, received)


def solution(mesh):
    return jax.shard_map(
        functools.partial(on_device, mesh.shape["gx"], mesh.shape["gy"]),
        mesh=mesh,
        in_specs=(
            P(None, "gx", "gy", None),
            P(None, "gx", "gy"),
            P("gx", "gy"),
            P("gx", "gy"),
            P(None, "gx", "gy"),
            P("gx", "gy"),
            P("gx", "gy"),
        ),
        out_specs=(P(None, "gx", "gy"), P(None, "gx", "gy", None)),
        check_vma=False,
    )
```

```python
import functools

import jax
import jax.numpy as jnp
import numpy as np
from jax import lax
from jax.experimental import pallas as pl
from jax.experimental.pallas import tpu as pltpu
from jax.sharding import PartitionSpec as P

VELOCITIES = (
    (0, 0, 0),
    (1, 0, 0),
    (-1, 0, 0),
    (0, 1, 0),
    (0, -1, 0),
    (0, 0, 1),
    (0, 0, -1),
    (1, 1, 0),
    (-1, -1, 0),
    (1, -1, 0),
    (-1, 1, 0),
    (1, 0, 1),
    (-1, 0, -1),
    (1, 0, -1),
    (-1, 0, 1),
    (0, 1, 1),
    (0, -1, -1),
    (0, 1, -1),
    (0, -1, 1),
)
Q = 19
FACE = 1.0 / 18.0
EDGE = 1.0 / 36.0
relaxation = 0.8
friction_rate = 8.0
screening = 0.25
softening = 0.25
gauss_term = 0.28209479177387814

STRETCH = 0.45
ERFCX = (
    0.2538730335007913,
    0.2542496247938967,
    0.22382455836296578,
    0.20419679225971624,
    0.007848770232788184,
    0.247605942768305,
    -0.264920441150418,
    0.07332591039690019,
)

PLANES = 8
ROWS = 16
LENGTH = 512
BLOCKS = 16
LANES = 128
SHELL = 6
SPAN = LENGTH // BLOCKS
NODES = PLANES * ROWS
WINDOW = 160

X_UP = tuple(q for q in range(Q) if VELOCITIES[q][0] == 1)
X_DOWN = tuple(q for q in range(Q) if VELOCITIES[q][0] == -1)
Y_UP = tuple(q for q in range(Q) if VELOCITIES[q][1] == 1)
Y_DOWN = tuple(q for q in range(Q) if VELOCITIES[q][1] == -1)
VMEM = pltpu.VMEM
WHOLE = pl.BlockSpec(memory_space=pltpu.VMEM)
SCALARS = pl.BlockSpec(memory_space=pltpu.SMEM)
UNREAD = pl.BlockSpec(memory_space=pl.ANY)
FAR = pl.BlockSpec(memory_space=pltpu.HBM)


def params(mib):
    return pltpu.CompilerParams(vmem_limit_bytes=mib * 1024 * 1024)


def f32(*shape):
    return jax.ShapeDtypeStruct(shape, jnp.float32)


def moments_of(pops):
    rho = pops[0]
    for q in range(1, Q):
        rho = rho + pops[q]
    momentum = []
    for d in range(3):
        total = None
        for q in range(Q):
            sign = VELOCITIES[q][d]
            if sign == 0:
                continue
            if total is None:
                total = pops[q]
            elif sign > 0:
                total = total + pops[q]
            else:
                total = total - pops[q]
        momentum.append(total)
    return rho, momentum


def start_kernel(
    base_ref,
    count_ref,
    cell_hbm,
    frac_hbm,
    charge_hbm,
    velocity_hbm,
    pop_hbm,
    send_x,
    send_y,
    send_corner,
    bead_ref,
    flow_ref,
    cell_ref,
    frac_ref,
    charge_ref,
    velocity_ref,
    pop,
    bead_sems,
    pop_sems,
):
    copies = [
        pltpu.make_async_copy(source, target, bead_sems.at[n])
        for n, (source, target) in enumerate(
            (
                (cell_hbm, cell_ref),
                (frac_hbm, frac_ref),
                (charge_hbm, charge_ref),
                (velocity_hbm, velocity_ref),
            )
        )
    ]
    loads = [
        pltpu.make_async_copy(pop_hbm.at[:, p], pop.at[:, p], pop_sems.at[p]) for p in range(PLANES)
    ]
    for copy in copies + loads:
        copy.start()
    block = lax.broadcasted_iota(jnp.int32, (BLOCKS, LANES), 0)
    lane = lax.broadcasted_iota(jnp.int32, (BLOCKS, LANES), 1)
    counts = jnp.zeros((BLOCKS, LANES), jnp.int32)
    for c in range(BLOCKS):
        counts = jnp.where(block == c, count_ref[c], counts)
    live = (lane < counts).astype(jnp.float32)
    for copy in copies:
        copy.wait()
    cell = cell_ref[...]
    first = lax.shift_right_logical(cell, 13)
    second = lax.shift_right_logical(cell, 9) & 15
    third = cell & 511
    start_first = base_ref[0]
    start_second = base_ref[1]
    start_third = block * SPAN
    x = (start_first + first).astype(jnp.float32) + frac_ref[0]
    y = (start_second + second).astype(jnp.float32) + frac_ref[1]
    z = third.astype(jnp.float32) + frac_ref[2]
    x = x - start_first.astype(jnp.float32)
    y = y - start_second.astype(jnp.float32)
    z = z - start_third.astype(jnp.float32)
    for k, value in enumerate((x, y, z, charge_ref[...] * live)):
        send_x[3 * ROWS :, k * LANES : (k + 1) * LANES] = value
        send_y[3 * PLANES :, k * LANES : (k + 1) * LANES] = value
    drags = (
        first.astype(jnp.float32),
        second.astype(jnp.float32),
        (third - start_third).astype(jnp.float32),
        frac_ref[0],
        frac_ref[1],
        frac_ref[2],
        velocity_ref[0],
        velocity_ref[1],
        velocity_ref[2],
        live,
    )
    for k, value in enumerate(drags):
        bead_ref[k] = value
    send_corner[...] = jnp.zeros_like(send_corner)
    for p in range(PLANES):
        loads[p].wait()
        rho, momentum = moments_of([pop[q, p] for q in range(Q)])
        inverse = 1.0 / rho
        for d in range(3):
            flow = momentum[d] * inverse
            flow_ref[d, p * ROWS : (p + 1) * ROWS, :] = flow
            send_y[d * PLANES + p : d * PLANES + p + 1, :] = flow[0:1]
            if p == 0:
                send_x[d * ROWS : (d + 1) * ROWS, :] = flow
                send_corner[d : d + 1, :] = flow[0:1]


def start(base, count, *arrays):
    far = [pltpu.with_memory_space_constraint(array, pltpu.HBM) for array in arrays]
    return pl.pallas_call(
        start_kernel,
        out_shape=(
            f32(3 * ROWS + BLOCKS, LENGTH),
            f32(3 * PLANES + BLOCKS, LENGTH),
            f32(8, LENGTH),
            f32(10, BLOCKS, LANES),
            f32(3, NODES, LENGTH),
        ),
        in_specs=[SCALARS] * 2 + [FAR] * 5,
        out_specs=(WHOLE,) * 5,
        scratch_shapes=[
            VMEM((BLOCKS, LANES), jnp.int32),
            VMEM((3, BLOCKS, LANES), jnp.float32),
            VMEM((BLOCKS, LANES), jnp.float32),
            VMEM((3, BLOCKS, LANES), jnp.float32),
            VMEM((Q, PLANES, ROWS, LENGTH), jnp.float32),
            pltpu.SemaphoreType.DMA((4,)),
            pltpu.SemaphoreType.DMA((PLANES,)),
        ],
        compiler_params=params(20),
        cost_estimate=pl.CostEstimate(flops=4000000, bytes_accessed=6000000, transcendentals=0),
        name="start",
    )(base, count, *far)


def radial_of(s):
    r = lax.rsqrt(s)
    rr = s * r
    below = 1.0 + (STRETCH * screening) * rr
    t = pl.reciprocal(below, approx=True)
    t = t * (2.0 - below * t)
    poly = jnp.full_like(t, ERFCX[-1])
    for coefficient in ERFCX[-2::-1]:
        poly = poly * t + coefficient
    decay = jnp.exp2(s * (-screening * screening * 1.4426950408889634))
    return decay * (poly * t * r + gauss_term) * (r * r)


def pair_blocks(kind, start, stop, codes_ref, cand_ref, own_ref, react_ref, wide_ref, acc):
    def block(c, carry):
        n = c - start
        acc[n] = jnp.zeros((3, LANES, LANES), jnp.float32)
        for s in range(SHELL):
            code = codes_ref[s, c]

            @pl.when(lax.shift_right_logical(code, 4) == kind)
            def _():
                e = code & 15
                steps = e - c
                steps = jnp.where(steps > 1, steps - BLOCKS, steps)
                steps = jnp.where(steps < -1, steps + BLOCKS, steps)
                shift_third = (steps * SPAN).astype(jnp.float32)
                xj, yj, zj, qj = (cand_ref[k, pl.ds(e, 1), :] for k in range(4))
                zj = zj + shift_third
                xj, yj, zj, qj = (jnp.broadcast_to(v, (8, LANES)) for v in (xj, yj, zj, qj))
                j = lax.broadcasted_iota(jnp.int32, (8, LANES), 1)
                j = j - lax.broadcasted_iota(jnp.int32, (8, LANES), 0) + LANES * jnp.abs(steps)
                sums = [jnp.zeros((8, LANES), jnp.float32) for _ in range(3)]
                for g in range(LANES // 8):
                    rows = slice(8 * g, 8 * g + 8)
                    dx = wide_ref[c, 0, rows] - xj
                    dy = wide_ref[c, 1, rows] - yj
                    dz = wide_ref[c, 2, rows] - zj
                    squares = dx * dx + dy * dy + dz * dz + softening
                    strength = wide_ref[c, 3, rows] * qj * radial_of(squares)
                    if kind == 0:
                        strength = jnp.where(j == 8 * g, 0.0, strength)
                    for d, delta in enumerate((dx, dy, dz)):
                        force = strength * delta
                        acc[n, d, rows] = acc[n, d, rows] + force
                        sums[d] = sums[d] + force
                for d in range(3):
                    total = jnp.sum(sums[d], axis=0, keepdims=True)
                    react_ref[d, pl.ds(e, 1), :] = react_ref[d, pl.ds(e, 1), :] - total

        return carry

    lax.fori_loop(start, stop, block, 0)
    j = lax.broadcasted_iota(jnp.int32, (8, LANES), 1)
    j = j - lax.broadcasted_iota(jnp.int32, (8, LANES), 0)
    for c in range(start, stop):
        for d in range(3):
            own = jnp.zeros((8, LANES), jnp.float32)
            for g in range(LANES // 8):
                column = jnp.sum(acc[c - start, d, 8 * g : 8 * g + 8], axis=1, keepdims=True)
                own = own + jnp.where(j == 8 * g, column, 0.0)
            own = jnp.sum(own, axis=0, keepdims=True)
            own_ref[d, c : c + 1, :] = own_ref[d, c : c + 1, :] + own


def gather_cand(cand, source, start, shift_first, shift_second):
    for k, shift in enumerate((shift_first, shift_second, 0.0, 0.0)):
        cand[k] = source[start:, k * LANES : (k + 1) * LANES] + shift


def pair_a_kernel(stop, codes_ref, source, flow_ref, own_ref, wide_ref, turned_ref, cand, acc):
    gather_cand(cand, source, 3 * ROWS, 0.0, 0.0)
    for d in range(3):
        for j in range(LENGTH // LANES):
            lanes = slice(j * LANES, (j + 1) * LANES)
            turned_ref[d, lanes, :] = flow_ref[d, :, lanes].T
    columns = [cand[k].T for k in range(4)]
    for c in range(BLOCKS):
        for k in range(4):
            wide_ref[c, k] = jnp.broadcast_to(columns[k][:, c : c + 1], (LANES, LANES))
    own_ref[...] = jnp.zeros_like(own_ref)
    pair_blocks(0, 0, stop, codes_ref, cand, own_ref, own_ref, wide_ref, acc)


def pair_b_kernel(
    codes_ref, source, wide_ref, turned_ref, own_ref, react_ref, field_ref, cand, acc
):
    for d in range(3):
        for j in range(LENGTH // LANES):
            lanes = slice(j * LANES, (j + 1) * LANES)
            field_ref[d, :, lanes] = turned_ref[d, lanes, :].T
    gather_cand(cand, source, 3 * ROWS, float(PLANES), 0.0)
    own_ref[...] = jnp.zeros_like(own_ref)
    react_ref[...] = jnp.zeros_like(react_ref)
    pair_blocks(1, 0, BLOCKS, codes_ref, cand, own_ref, react_ref, wide_ref, acc)


def pair_c_kernel(codes_ref, source, wide_ref, after_ref, own_ref, react_ref, cand, acc):
    del after_ref
    gather_cand(cand, source, 3 * PLANES, 0.0, float(ROWS))
    own_ref[...] = jnp.zeros_like(own_ref)
    react_ref[...] = jnp.zeros_like(react_ref)
    pair_blocks(2, 0, BLOCKS, codes_ref, cand, own_ref, react_ref, wide_ref, acc)


def pair_d_kernel(start, codes_ref, source, wide_ref, after_ref, own_ref, cand, acc):
    del after_ref
    gather_cand(cand, source, 3 * ROWS, 0.0, 0.0)
    own_ref[...] = jnp.zeros_like(own_ref)
    pair_blocks(0, start, BLOCKS, codes_ref, cand, own_ref, own_ref, wide_ref, acc)


def pair_cost(tiles):
    return pl.CostEstimate(
        flops=1000000 * tiles, bytes_accessed=1000000, transcendentals=50000 * tiles
    )


def pair_scratch(blocks):
    return [
        VMEM((4, BLOCKS, LANES), jnp.float32),
        VMEM((blocks, 3, LANES, LANES), jnp.float32),
    ]


BEADS = f32(3, BLOCKS, LANES)


def pair_a(stop, codes, own, flow):
    return pl.pallas_call(
        functools.partial(pair_a_kernel, stop),
        out_shape=(BEADS, f32(BLOCKS, 4, LANES, LANES), f32(3, LENGTH, NODES)),
        in_specs=[SCALARS] + [WHOLE] * 2,
        out_specs=(WHOLE,) * 3,
        scratch_shapes=pair_scratch(stop),
        compiler_params=params(20),
        cost_estimate=pair_cost(2 * stop),
        name="pair_a",
    )(codes, own, flow)


def pair_b(codes, following, wide, field):
    return pl.pallas_call(
        pair_b_kernel,
        out_shape=(BEADS, BEADS, f32(3, NODES, LENGTH)),
        in_specs=[SCALARS] + [WHOLE] * 3,
        out_specs=(WHOLE,) * 3,
        scratch_shapes=pair_scratch(BLOCKS),
        compiler_params=params(20),
        cost_estimate=pair_cost(40),
        name="pair_b",
    )(codes, following, wide, field)


def pair_c(codes, side, wide, after):
    return pl.pallas_call(
        pair_c_kernel,
        out_shape=(BEADS, BEADS),
        in_specs=[SCALARS] + [WHOLE] * 2 + [UNREAD],
        out_specs=(WHOLE,) * 2,
        scratch_shapes=pair_scratch(BLOCKS),
        compiler_params=params(20),
        cost_estimate=pair_cost(40),
        name="pair_c",
    )(codes, side, wide, after)


def pair_d(start, codes, own, wide, after):
    return pl.pallas_call(
        functools.partial(pair_d_kernel, start),
        out_shape=BEADS,
        in_specs=[SCALARS] + [WHOLE] * 2 + [UNREAD],
        out_specs=WHOLE,
        scratch_shapes=pair_scratch(BLOCKS - start),
        compiler_params=params(20),
        cost_estimate=pair_cost(2 * (BLOCKS - start)),
        name="pair_d",
    )(codes, own, wide, after)


def hat(steps, fraction):
    return jnp.where(steps == 0.0, 1.0 - fraction, jnp.where(steps == 1.0, fraction, 0.0))


def node_first(k):
    value = jnp.where(k < NODES, lax.shift_right_logical(k, 4), PLANES)
    value = jnp.where(k < NODES + ROWS, value, k - (NODES + ROWS))
    value = jnp.where(k < NODES + ROWS + PLANES, value, PLANES)
    return jnp.where(k < NODES + ROWS + PLANES + 1, value, -8).astype(jnp.float32)


def node_second(k):
    value = jnp.where(k < NODES + ROWS, k & 15, ROWS)
    return jnp.where(k < NODES + ROWS + PLANES + 1, value, -8).astype(jnp.float32)


def halves(value):
    high = value.astype(jnp.bfloat16)
    low = (value - high.astype(jnp.float32)).astype(jnp.bfloat16)
    return high, low


def product(left, right, dims):
    left_high, left_low = left
    right_high, right_low = right
    dot = functools.partial(
        lax.dot_general, dimension_numbers=(dims, ((), ())), preferred_element_type=jnp.float32
    )
    return dot(left_high, right_high) + (dot(left_low, right_high) + dot(left_high, right_low))


DEEP = 48


def friction_kernel(
    bead_ref,
    turned_ref,
    from_next,
    from_side,
    corner_ref,
    drag_ref,
    field_ref,
    ghost_x,
    ghost_y,
    ghost_corner_ref,
    flow_high,
    flow_low,
    total_ref,
):
    extra = WINDOW - NODES
    k_row = lax.broadcasted_iota(jnp.int32, (WINDOW, 1), 0)
    first_row, second_row = node_first(k_row), node_second(k_row)
    depth = lax.broadcasted_iota(jnp.int32, (DEEP, 1), 0).astype(jnp.float32)
    padding = jnp.zeros((extra - ROWS - PLANES - 1, LANES), jnp.float32)
    total_ref[...] = jnp.zeros_like(total_ref)
    for d in range(3):
        for j in range(LENGTH // LANES):
            lanes = slice(j * LANES, (j + 1) * LANES)
            beside = jnp.concatenate(
                [
                    from_next[d * ROWS : (d + 1) * ROWS, lanes],
                    from_side[d * PLANES : (d + 1) * PLANES, lanes],
                    corner_ref[d : d + 1, lanes],
                    padding,
                ],
                axis=0,
            ).T
            high, low = halves(turned_ref[d, lanes, :])
            high_beside, low_beside = halves(beside)
            flow_high[d, lanes, 0:NODES] = high
            flow_low[d, lanes, 0:NODES] = low
            flow_high[d, lanes, NODES:WINDOW] = high_beside
            flow_low[d, lanes, NODES:WINDOW] = low_beside
        flow_high[d, LENGTH : LENGTH + 16, :] = flow_high[d, 0:16, :]
        flow_low[d, LENGTH : LENGTH + 16, :] = flow_low[d, 0:16, :]

    for c in range(BLOCKS):
        span = slice(c * SPAN, c * SPAN + DEEP)
        rows = [bead_ref[k, c : c + 1] for k in range(10)]
        weight = halves(
            hat(first_row - rows[0], rows[3]) * hat(second_row - rows[1], rows[4])
        )
        along = hat(depth - rows[2], rows[5])
        nodes = tuple(
            jnp.concatenate([part[d, span, :] for d in range(3)], axis=0)
            for part in (flow_high, flow_low)
        )
        fluid = product(nodes, weight, ((1,), (0,)))
        pushes = []
        for d in range(3):
            here = jnp.sum(fluid[d * DEEP : (d + 1) * DEEP] * along, axis=0, keepdims=True)
            drag = friction_rate * (here - rows[6 + d]) * rows[9]
            drag_ref[d, c : c + 1, :] = drag
            pushes.append(along * -drag)
        spread = product(halves(jnp.concatenate(pushes, axis=0)), weight, ((1,), (1,)))
        for d in range(3):
            total_ref[d, span, 0:WINDOW] = (
                total_ref[d, span, 0:WINDOW] + spread[d * DEEP : (d + 1) * DEEP]
            )
    ghost_corner_ref[...] = jnp.zeros_like(ghost_corner_ref)
    for d in range(3):
        total_ref[d, 0:16, :] = total_ref[d, 0:16, :] + total_ref[d, LENGTH : LENGTH + 16, :]
        field_ref[d] = total_ref[d, 0:LENGTH, 0:NODES]
        for j in range(LENGTH // LANES):
            lanes = slice(j * LANES, (j + 1) * LANES)
            beside = total_ref[d, lanes, NODES : NODES + LANES].T
            ghost_x[d * ROWS : (d + 1) * ROWS, lanes] = beside[0:ROWS]
            ghost_y[d * PLANES : (d + 1) * PLANES, lanes] = beside[ROWS : ROWS + PLANES]
            ghost_corner_ref[d : d + 1, lanes] = beside[ROWS + PLANES : ROWS + PLANES + 1]


def friction(beads, turned, following, side, corner):
    return pl.pallas_call(
        friction_kernel,
        out_shape=(
            f32(3, BLOCKS, LANES),
            f32(3, LENGTH, NODES),
            f32(3 * ROWS, LENGTH),
            f32(3 * PLANES, LENGTH),
            f32(8, LENGTH),
        ),
        in_specs=[WHOLE] * 5,
        out_specs=(WHOLE,) * 5,
        scratch_shapes=[
            VMEM((3, LENGTH + 16, WINDOW), jnp.bfloat16),
            VMEM((3, LENGTH + 16, WINDOW), jnp.bfloat16),
            VMEM((3, LENGTH + 16, 2 * LANES), jnp.float32),
        ],
        compiler_params=params(24),
        cost_estimate=pl.CostEstimate(flops=60000000, bytes_accessed=3000000, transcendentals=0),
        name="friction",
    )(beads, turned, following, side, corner)


def relaxed_of(p, wanted, pop, field_ref, ghost_x, ghost_y, corner_ref):
    row_index = lax.broadcasted_iota(jnp.int32, (ROWS, LENGTH), 0)
    rho, momentum = moments_of([pop[q, p] for q in range(Q)])
    inverse = 1.0 / rho
    velocity = []
    for d in range(3):
        force = field_ref[d, p * ROWS : (p + 1) * ROWS]
        edge = ghost_y[d * PLANES + p : d * PLANES + p + 1]
        if p == 0:
            force = force + ghost_x[d * ROWS : (d + 1) * ROWS]
            edge = edge + corner_ref[d : d + 1]
        force = force + jnp.where(row_index == 0, edge, 0.0)
        velocity.append((momentum[d] + relaxation * force) * inverse)
    speed = velocity[0] * velocity[0] + velocity[1] * velocity[1] + velocity[2] * velocity[2]
    base = 1.0 - 1.5 * speed
    weights = (rho * (1.25 / 3.0), rho * (1.25 * FACE), rho * (1.25 * EDGE))
    for q in wanted:
        cx, cy, cz = VELOCITIES[q]
        moving = abs(cx) + abs(cy) + abs(cz)
        equilibrium = base
        if moving:
            projected = None
            for sign, component in zip((cx, cy, cz), velocity):
                if sign == 0:
                    continue
                if projected is None:
                    projected = component if sign > 0 else -component
                elif sign > 0:
                    projected = projected + component
                else:
                    projected = projected - component
            equilibrium = base + projected * (3.0 + 4.5 * projected)
        relaxed = weights[moving] * equilibrium - 0.25 * pop[q, p]
        if cz:
            relaxed = pltpu.roll(relaxed, cz % LENGTH, 1)
        if cy:
            relaxed = pltpu.roll(relaxed, cy % ROWS, 0)
        yield q, relaxed


def faces_kernel(pop, field_ref, ghost_x, ghost_y, corner_ref, react_ref, x_up, x_down):
    for d in range(3):
        x_up[5 * ROWS :, d * LANES : (d + 1) * LANES] = react_ref[d]
    x_up[5 * ROWS :, 3 * LANES :] = jnp.zeros((BLOCKS, LANES), jnp.float32)
    for p, group, face in ((PLANES - 1, X_UP, x_up), (0, X_DOWN, x_down)):
        for q, relaxed in relaxed_of(p, group, pop, field_ref, ghost_x, ghost_y, corner_ref):
            n = group.index(q)
            face[n * ROWS : (n + 1) * ROWS, :] = relaxed


def faces(populations, field, ghost_x, ghost_y, corner, react):
    return pl.pallas_call(
        faces_kernel,
        out_shape=(f32(5 * ROWS + BLOCKS, LENGTH), f32(5 * ROWS, LENGTH)),
        in_specs=[WHOLE] * 6,
        out_specs=(WHOLE,) * 2,
        compiler_params=params(24),
        cost_estimate=pl.CostEstimate(flops=2000000, bytes_accessed=2000000, transcendentals=0),
        name="faces",
    )(populations, field, ghost_x, ghost_y, corner, react)


def collide_kernel(
    pop,
    field_ref,
    ghost_x,
    ghost_y,
    corner_ref,
    after_ref,
    out_hbm,
    y_up,
    y_down,
    tiles_up,
    tiles_down,
    out,
    out_sems,
):
    del after_ref

    def store(p):
        return pltpu.make_async_copy(out.at[:, p], out_hbm.at[:, p], out_sems.at[p])

    for p in range(PLANES):
        for q, relaxed in relaxed_of(p, range(Q), pop, field_ref, ghost_x, ghost_y, corner_ref):
            cx, cy, unused = VELOCITIES[q]
            target = (p + cx) % PLANES
            out[q, target] = relaxed
            if cy == 1:
                n = Y_UP.index(q)
                y_up[n, target : target + 1, :] = relaxed[0:1]
                tiles_up[n, target] = relaxed[0:8]
            if cy == -1:
                n = Y_DOWN.index(q)
                y_down[n, target : target + 1, :] = relaxed[ROWS - 1 : ROWS]
                tiles_down[n, target] = relaxed[8:16]
        if 2 <= p:
            store(p - 1).start()
    store(0).start()
    store(PLANES - 1).start()
    for p in range(PLANES):
        store(p).wait()


def collide(populations, field, ghost_x, ghost_y, corner, after):
    return pl.pallas_call(
        collide_kernel,
        out_shape=(
            f32(Q, PLANES, ROWS, LENGTH),
            f32(5, PLANES, LENGTH),
            f32(5, PLANES, LENGTH),
            f32(5, PLANES, 8, LENGTH),
            f32(5, PLANES, 8, LENGTH),
        ),
        in_specs=[WHOLE] * 5 + [UNREAD],
        out_specs=(FAR,) + (WHOLE,) * 4,
        scratch_shapes=[
            VMEM((Q, PLANES, ROWS, LENGTH), jnp.float32),
            pltpu.SemaphoreType.DMA((PLANES,)),
        ],
        compiler_params=params(32),
        cost_estimate=pl.CostEstimate(flops=20000000, bytes_accessed=12000000, transcendentals=0),
        name="collide",
    )(populations, field, ghost_x, ghost_y, corner, after)


def forward_kernel(x_up, x_down, react_ref, up_ref, down_ref):
    up_ref[...] = jnp.zeros_like(up_ref)
    down_ref[...] = jnp.zeros_like(down_ref)
    for d in range(3):
        up_ref[8:, d * LANES : (d + 1) * LANES] = react_ref[d]
    rows = [X_UP.index(7) * ROWS, X_DOWN.index(10) * ROWS]
    up_ref[0:1, :] = x_up[rows[0] : rows[0] + 1, :]
    up_ref[1:2, :] = x_down[rows[1] : rows[1] + 1, :]
    rows = [X_UP.index(9) * ROWS + ROWS - 1, X_DOWN.index(8) * ROWS + ROWS - 1]
    down_ref[0:1, :] = x_up[rows[0] : rows[0] + 1, :]
    down_ref[1:2, :] = x_down[rows[1] : rows[1] + 1, :]


def forward(x_up, x_down, react):
    return pl.pallas_call(
        forward_kernel,
        out_shape=(f32(8 + BLOCKS, LENGTH), f32(8, LENGTH)),
        in_specs=[WHOLE] * 3,
        out_specs=(WHOLE,) * 2,
        compiler_params=params(8),
        name="forward",
    )(x_up, x_down, react)


def finish_kernel(
    out_in,
    x_up,
    x_down,
    y_up,
    y_down,
    tiles_up,
    tiles_down,
    from_below,
    from_above,
    drag_ref,
    own_a,
    own_b,
    own_c,
    own_d,
    out_hbm,
    force_ref,
    tiles,
    faces,
    tile_sems,
    face_sems,
):
    del out_in
    copies = []
    for end, (group, received, plane) in enumerate(((X_UP, x_up, 0), (X_DOWN, x_down, PLANES - 1))):
        for n, q in enumerate(group):
            cy = VELOCITIES[q][1]
            faces[end, n] = received[n * ROWS : (n + 1) * ROWS]
            rows = pl.ds((0, 8, 0)[cy], ROWS if cy == 0 else 8)
            copies.append(
                pltpu.make_async_copy(
                    faces.at[end, n, rows], out_hbm.at[q, plane, rows], face_sems.at[end, n]
                )
            )
            copies[-1].start()
    corners = {7: from_below[0:1], 10: from_below[1:2], 9: from_above[0:1], 8: from_above[1:2]}
    row_index = lax.broadcasted_iota(jnp.int32, (8, LENGTH), 0)
    sides = ((Y_UP, y_up, tiles_up, 0), (Y_DOWN, y_down, tiles_down, 8))
    for side, (group, received, local, start) in enumerate(sides):
        row = 0 if side == 0 else 7
        for n, q in enumerate(group):
            cx = VELOCITIES[q][0]
            for p in range(PLANES):
                edge, inner = received[n, p : p + 1, :], local[n, p]
                if cx == 1 and p == 0:
                    first = X_UP.index(q) * ROWS + start
                    edge, inner = corners[q], x_up[first : first + 8]
                if cx == -1 and p == PLANES - 1:
                    first = X_DOWN.index(q) * ROWS + start
                    edge, inner = corners[q], x_down[first : first + 8]
                tiles[side, n, p] = jnp.where(row_index == row, edge, inner)
            copies.append(
                pltpu.make_async_copy(
                    tiles.at[side, n], out_hbm.at[q, :, pl.ds(start, 8)], tile_sems.at[side, n]
                )
            )
            copies[-1].start()
    for d in range(3):
        lanes = slice(d * LANES, (d + 1) * LANES)
        own = own_a[d] + own_b[d] + own_c[d] + own_d[d]
        back = x_up[5 * ROWS :, lanes] + from_below[8:, lanes]
        force_ref[d] = own + back + drag_ref[d]
    for copy in copies:
        copy.wait()


def finish(out, *received):
    return pl.pallas_call(
        finish_kernel,
        out_shape=(f32(Q, PLANES, ROWS, LENGTH), f32(3, BLOCKS, LANES)),
        in_specs=[FAR] + [WHOLE] * 13,
        out_specs=(FAR, WHOLE),
        scratch_shapes=[
            VMEM((2, 5, PLANES, 8, LENGTH), jnp.float32),
            VMEM((2, 5, ROWS, LENGTH), jnp.float32),
            pltpu.SemaphoreType.DMA((2, 5)),
            pltpu.SemaphoreType.DMA((2, 5)),
        ],
        input_output_aliases={0: 0},
        compiler_params=params(16),
        cost_estimate=pl.CostEstimate(flops=1000, bytes_accessed=8000000, transcendentals=0),
        name="finish",
    )(out, *received)


CUT = 10


def on_device(n_first, n_second, populations, frac, cell, charge, velocity, count, codes):
    def to(value, steps_first, steps_second):
        pairs = [
            (
                i * n_second + j,
                ((i + steps_first) % n_first) * n_second + (j + steps_second) % n_second,
            )
            for i in range(n_first)
            for j in range(n_second)
        ]
        return lax.ppermute(value, ("gx", "gy"), pairs)

    base = jnp.stack([lax.axis_index("gx") * PLANES, lax.axis_index("gy") * ROWS]).astype(jnp.int32)
    count, codes = count.reshape(BLOCKS), codes.T
    own, side, corner, beads, flow = start(base, count, cell, frac, charge, velocity, populations)
    following, side, corner = to(own, -1, 0), to(side, 0, -1), to(corner, -1, -1)
    own_a, wide, turned = pair_a(CUT, codes, own, flow)
    drag, turned, ghost_x, ghost_y, corner = friction(beads, turned, following, side, corner)
    ghost_x, ghost_y, corner = to(ghost_x, 1, 0), to(ghost_y, 0, 1), to(corner, 1, 1)
    own_b, react, field = pair_b(codes, following, wide, turned)
    x_up, x_down = faces(populations, field, ghost_x, ghost_y, corner, react)
    out, y_up, y_down, tiles_up, tiles_down = collide(
        populations, field, ghost_x, ghost_y, corner, x_up
    )
    x_up, x_down = to(x_up, 1, 0), to(x_down, -1, 0)
    y_up, y_down = to(y_up, 0, 1), to(y_down, 0, -1)
    own_c, react = pair_c(codes, side, wide, tiles_up)
    up, down = forward(x_up, x_down, react)
    from_below, from_above = to(up, 0, 1), to(down, 0, -1)
    own_d = pair_d(CUT, codes, own, wide, up)
    out, force = finish(
        out,
        x_up,
        x_down,
        y_up,
        y_down,
        tiles_up,
        tiles_down,
        from_below,
        from_above,
        drag,
        own_a,
        own_b,
        own_c,
        own_d,
    )
    return force, out


def solution(mesh):
    return jax.shard_map(
        functools.partial(on_device, mesh.shape["gx"], mesh.shape["gy"]),
        mesh=mesh,
        in_specs=(
            P(None, "gx", "gy", None),
            P(None, "gx", "gy"),
            P("gx", "gy"),
            P("gx", "gy"),
            P(None, "gx", "gy"),
            P("gx", "gy"),
            P("gx", "gy"),
        ),
        out_specs=(P(None, "gx", "gy"), P(None, "gx", "gy", None)),
        check_vma=False,
    )
```

```python
import functools

import jax
import jax.numpy as jnp
import numpy as np
from jax import lax
from jax.experimental import pallas as pl
from jax.experimental.pallas import tpu as pltpu
from jax.sharding import PartitionSpec as P

VELOCITIES = (
    (0, 0, 0),
    (1, 0, 0),
    (-1, 0, 0),
    (0, 1, 0),
    (0, -1, 0),
    (0, 0, 1),
    (0, 0, -1),
    (1, 1, 0),
    (-1, -1, 0),
    (1, -1, 0),
    (-1, 1, 0),
    (1, 0, 1),
    (-1, 0, -1),
    (1, 0, -1),
    (-1, 0, 1),
    (0, 1, 1),
    (0, -1, -1),
    (0, 1, -1),
    (0, -1, 1),
)
Q = 19
FACE = 1.0 / 18.0
EDGE = 1.0 / 36.0
relaxation = 0.8
friction_rate = 8.0
screening = 0.25
softening = 0.25
gauss_term = 0.28209479177387814

STRETCH = 0.45
ERFCX = (
    0.2538730335007913,
    0.2542496247938967,
    0.22382455836296578,
    0.20419679225971624,
    0.007848770232788184,
    0.247605942768305,
    -0.264920441150418,
    0.07332591039690019,
)

PLANES = 8
ROWS = 16
LENGTH = 512
BLOCKS = 16
LANES = 128
SHELL = 6
SPAN = LENGTH // BLOCKS
NODES = PLANES * ROWS
WINDOW = 160

X_UP = tuple(q for q in range(Q) if VELOCITIES[q][0] == 1)
X_DOWN = tuple(q for q in range(Q) if VELOCITIES[q][0] == -1)
Y_UP = tuple(q for q in range(Q) if VELOCITIES[q][1] == 1)
Y_DOWN = tuple(q for q in range(Q) if VELOCITIES[q][1] == -1)
VMEM = pltpu.VMEM
WHOLE = pl.BlockSpec(memory_space=pltpu.VMEM)
UNREAD = pl.BlockSpec(memory_space=pl.ANY)
FAR = pl.BlockSpec(memory_space=pltpu.HBM)


RUN = 32


def is_late():
    return lax.axis_index("gx") % RUN <= 1


def is_odd():
    return lax.axis_index("gx") % 2 == 1


def params(mib):
    return pltpu.CompilerParams(vmem_limit_bytes=mib * 1024 * 1024)


def f32(*shape):
    return jax.ShapeDtypeStruct(shape, jnp.float32)


def moments_of(pops):
    rho = pops[0]
    for q in range(1, Q):
        rho = rho + pops[q]
    momentum = []
    for d in range(3):
        total = None
        for q in range(Q):
            sign = VELOCITIES[q][d]
            if sign == 0:
                continue
            if total is None:
                total = pops[q]
            elif sign > 0:
                total = total + pops[q]
            else:
                total = total - pops[q]
        momentum.append(total)
    return rho, momentum


def start_kernel(
    count_hbm,
    cell_hbm,
    frac_hbm,
    charge_hbm,
    velocity_hbm,
    pop_hbm,
    send_x,
    send_y,
    send_corner,
    bead_ref,
    flow_ref,
    count_ref,
    cell_ref,
    frac_ref,
    charge_ref,
    velocity_ref,
    pop,
    bead_sems,
    pop_sems,
):
    copies = [
        pltpu.make_async_copy(source, target, bead_sems.at[n])
        for n, (source, target) in enumerate(
            (
                (count_hbm, count_ref),
                (cell_hbm, cell_ref),
                (frac_hbm, frac_ref),
                (charge_hbm, charge_ref),
                (velocity_hbm, velocity_ref),
            )
        )
    ]
    loads = [
        pltpu.make_async_copy(pop_hbm.at[:, p], pop.at[:, p], pop_sems.at[p]) for p in range(PLANES)
    ]
    for copy in copies + loads:
        copy.start()
    block = lax.broadcasted_iota(jnp.int32, (BLOCKS, LANES), 0)
    lane = lax.broadcasted_iota(jnp.int32, (BLOCKS, LANES), 1)
    counts = jnp.zeros((BLOCKS, LANES), jnp.int32)
    for copy in copies:
        copy.wait()
    for c in range(BLOCKS):
        counts = jnp.where(block == c, count_ref[c], counts)
    live = (lane < counts).astype(jnp.float32)
    cell = cell_ref[...]
    first = lax.shift_right_logical(cell, 13)
    second = lax.shift_right_logical(cell, 9) & 15
    third = cell & 511
    start_first = lax.axis_index("gx") * PLANES
    start_second = lax.axis_index("gy") * ROWS
    start_third = block * SPAN
    x = (start_first + first).astype(jnp.float32) + frac_ref[0]
    y = (start_second + second).astype(jnp.float32) + frac_ref[1]
    z = third.astype(jnp.float32) + frac_ref[2]
    x = x - start_first.astype(jnp.float32)
    y = y - start_second.astype(jnp.float32)
    z = z - start_third.astype(jnp.float32)
    for k, value in enumerate((x, y, z, charge_ref[...] * live)):
        send_x[3 * ROWS :, k * LANES : (k + 1) * LANES] = value
        send_y[3 * PLANES :, k * LANES : (k + 1) * LANES] = value
    drags = (
        first.astype(jnp.float32),
        second.astype(jnp.float32),
        (third - start_third).astype(jnp.float32),
        frac_ref[0],
        frac_ref[1],
        frac_ref[2],
        velocity_ref[0],
        velocity_ref[1],
        velocity_ref[2],
        live,
    )
    for k, value in enumerate(drags):
        bead_ref[k] = value
    send_corner[...] = jnp.zeros_like(send_corner)
    for p in range(PLANES):
        loads[p].wait()
        rho, momentum = moments_of([pop[q, p] for q in range(Q)])
        inverse = 1.0 / rho
        for d in range(3):
            flow = momentum[d] * inverse
            flow_ref[d, p * ROWS : (p + 1) * ROWS, :] = flow
            send_y[d * PLANES + p : d * PLANES + p + 1, :] = flow[0:1]
            if p == 0:
                send_x[d * ROWS : (d + 1) * ROWS, :] = flow
                send_corner[d : d + 1, :] = flow[0:1]


def start(*arrays):
    far = [pltpu.with_memory_space_constraint(array, pltpu.HBM) for array in arrays]
    return pl.pallas_call(
        start_kernel,
        out_shape=(
            f32(3 * ROWS + BLOCKS, LENGTH),
            f32(3 * PLANES + BLOCKS, LENGTH),
            f32(8, LENGTH),
            f32(10, BLOCKS, LANES),
            f32(3, NODES, LENGTH),
        ),
        in_specs=[FAR] * 6,
        out_specs=(WHOLE,) * 5,
        scratch_shapes=[
            pltpu.SMEM((BLOCKS,), jnp.int32),
            VMEM((BLOCKS, LANES), jnp.int32),
            VMEM((3, BLOCKS, LANES), jnp.float32),
            VMEM((BLOCKS, LANES), jnp.float32),
            VMEM((3, BLOCKS, LANES), jnp.float32),
            VMEM((Q, PLANES, ROWS, LENGTH), jnp.float32),
            pltpu.SemaphoreType.DMA((5,)),
            pltpu.SemaphoreType.DMA((PLANES,)),
        ],
        compiler_params=params(20),
        cost_estimate=pl.CostEstimate(flops=4000000, bytes_accessed=6000000, transcendentals=0),
        name="start",
    )(*far)


def radial_of(s):
    r = lax.rsqrt(s)
    rr = s * r
    below = 1.0 + (STRETCH * screening) * rr
    t = pl.reciprocal(below, approx=True)
    t = t * (2.0 - below * t)
    poly = jnp.full_like(t, ERFCX[-1])
    for coefficient in ERFCX[-2::-1]:
        poly = poly * t + coefficient
    decay = jnp.exp2(s * (-screening * screening * 1.4426950408889634))
    return decay * (poly * t * r + gauss_term) * (r * r)


def pair_tiles(kind, start, stop, codes_ref, cand_ref, react_ref, wide_ref, acc, base, listed):
    count = jnp.int32(0)
    for c in range(start, stop):
        for s in range(SHELL):
            code = codes_ref[s, c]
            listed[count] = (code & 15) + BLOCKS * c
            count = count + (lax.shift_right_logical(code, 4) == kind).astype(jnp.int32)

    def tile(i, carry):
        entry = listed[i]
        c = lax.shift_right_logical(entry, 4)
        e = entry & 15
        n = c - base
        steps = e - c
        steps = jnp.where(steps > 1, steps - BLOCKS, steps)
        steps = jnp.where(steps < -1, steps + BLOCKS, steps)
        shift_third = (steps * SPAN).astype(jnp.float32)
        xj, yj, zj, qj = (cand_ref[k, pl.ds(e, 1), :] for k in range(4))
        zj = zj + shift_third
        xj, yj, zj, qj = (jnp.broadcast_to(v, (8, LANES)) for v in (xj, yj, zj, qj))
        j = lax.broadcasted_iota(jnp.int32, (8, LANES), 1)
        j = j - lax.broadcasted_iota(jnp.int32, (8, LANES), 0) + LANES * jnp.abs(steps)
        sums = [jnp.zeros((8, LANES), jnp.float32) for _ in range(3)]
        for g in range(LANES // 8):
            rows = slice(8 * g, 8 * g + 8)
            dx = wide_ref[c, 0, rows] - xj
            dy = wide_ref[c, 1, rows] - yj
            dz = wide_ref[c, 2, rows] - zj
            squares = dx * dx + dy * dy + dz * dz + softening
            strength = wide_ref[c, 3, rows] * qj * radial_of(squares)
            if kind == 0:
                strength = jnp.where(j == 8 * g, 0.0, strength)
            for d, delta in enumerate((dx, dy, dz)):
                force = strength * delta
                acc[n, d, rows] = acc[n, d, rows] + force
                sums[d] = sums[d] + force
        for d in range(3):
            total = jnp.sum(sums[d], axis=0, keepdims=True)
            react_ref[d, pl.ds(e, 1), :] = react_ref[d, pl.ds(e, 1), :] - total
        return carry

    lax.fori_loop(0, count, tile, 0)


def copy_sums(acc_in, acc):
    def block(c, carry):
        acc[c] = acc_in[c]
        return carry

    lax.fori_loop(0, BLOCKS, block, 0)


def own_sums(start, stop, acc, base, own_ref):
    j = lax.broadcasted_iota(jnp.int32, (8, LANES), 1)
    j = j - lax.broadcasted_iota(jnp.int32, (8, LANES), 0)
    for c in range(start, stop):
        for d in range(3):
            own = jnp.zeros((8, LANES), jnp.float32)
            for g in range(LANES // 8):
                column = jnp.sum(acc[c - base, d, 8 * g : 8 * g + 8], axis=1, keepdims=True)
                own = own + jnp.where(j == 8 * g, column, 0.0)
            own = jnp.sum(own, axis=0, keepdims=True)
            own_ref[d, c : c + 1, :] = own_ref[d, c : c + 1, :] + own


def gather_cand(cand, source, start, shift_first, shift_second):
    for k, shift in enumerate((shift_first, shift_second, 0.0, 0.0)):
        cand[k] = source[start:, k * LANES : (k + 1) * LANES] + shift


def pair_a_kernel(
    stop,
    codes_hbm,
    source,
    flow_ref,
    own_ref,
    wide_ref,
    turned_ref,
    acc,
    cand,
    listed,
    codes_ref,
    codes_sem,
):
    codes = pltpu.make_async_copy(codes_hbm, codes_ref, codes_sem)
    codes.start()
    gather_cand(cand, source, 3 * ROWS, 0.0, 0.0)
    for d in range(3):
        for j in range(LENGTH // LANES):
            lanes = slice(j * LANES, (j + 1) * LANES)
            turned_ref[d, lanes, :] = flow_ref[d, :, lanes].T
    columns = [cand[k].T for k in range(4)]
    for c in range(BLOCKS):
        for k in range(4):
            wide_ref[c, k] = jnp.broadcast_to(columns[k][:, c : c + 1], (LANES, LANES))
    own_ref[...] = jnp.zeros_like(own_ref)

    def clear(c, carry):
        acc[c] = jnp.zeros((3, LANES, LANES), jnp.float32)
        return carry

    lax.fori_loop(0, BLOCKS, clear, 0)

    codes.wait()

    @pl.when(jnp.logical_not(is_late()))
    def _():
        pair_tiles(0, 0, stop, codes_ref, cand, own_ref, wide_ref, acc, 0, listed)


def pair_b_kernel(
    stop,
    codes_hbm,
    own_source,
    source,
    wide_ref,
    acc_in,
    turned_ref,
    own_ref,
    react_ref,
    acc,
    field_ref,
    cand,
    listed,
    codes_ref,
    codes_sem,
):
    codes = pltpu.make_async_copy(codes_hbm, codes_ref, codes_sem)
    codes.start()
    for d in range(3):
        for j in range(LENGTH // LANES):
            lanes = slice(j * LANES, (j + 1) * LANES)
            field_ref[d, :, lanes] = turned_ref[d, lanes, :].T
    own_ref[...] = jnp.zeros_like(own_ref)
    react_ref[...] = jnp.zeros_like(react_ref)
    copy_sums(acc_in, acc)
    gather_cand(cand, source, 3 * ROWS, float(PLANES), 0.0)
    codes.wait()
    pair_tiles(1, 0, BLOCKS, codes_ref, cand, react_ref, wide_ref, acc, 0, listed)

    @pl.when(is_late())
    def _():
        gather_cand(cand, own_source, 3 * ROWS, 0.0, 0.0)
        pair_tiles(0, 0, stop, codes_ref, cand, own_ref, wide_ref, acc, 0, listed)


def pair_c_kernel(
    codes_hbm,
    source,
    wide_ref,
    acc_in,
    after_ref,
    react_ref,
    acc,
    cand,
    listed,
    codes_ref,
    codes_sem,
):
    del after_ref
    codes = pltpu.make_async_copy(codes_hbm, codes_ref, codes_sem)
    codes.start()
    gather_cand(cand, source, 3 * PLANES, 0.0, float(ROWS))
    react_ref[...] = jnp.zeros_like(react_ref)
    copy_sums(acc_in, acc)
    codes.wait()
    pair_tiles(2, 0, BLOCKS, codes_ref, cand, react_ref, wide_ref, acc, 0, listed)


def last_kernel(
    start,
    out_in,
    codes_hbm,
    source,
    wide_ref,
    acc_in,
    own_a,
    own_b,
    after_ref,
    first_ref,
    second_ref,
    y_up,
    y_down,
    tiles_up,
    tiles_down,
    out_hbm,
    own_ref,
    corner_tiles,
    cand,
    listed,
    codes_ref,
    codes_sem,
    acc,
    tiles,
    faces,
    tile_sems,
    face_sems,
):
    del out_in, after_ref
    x_up = Faces(first_ref, second_ref, 0)
    x_down = Faces(first_ref, second_ref, 1)
    codes = pltpu.make_async_copy(codes_hbm, codes_ref, codes_sem)
    codes.start()
    copies = []
    for end, (group, received, plane) in enumerate(((X_UP, x_up, 0), (X_DOWN, x_down, PLANES - 1))):
        for n, q in enumerate(group):
            cy = VELOCITIES[q][1]
            faces[end, n] = received[n * ROWS : (n + 1) * ROWS]
            rows = pl.ds((0, 8, 0)[cy], ROWS if cy == 0 else 8)
            if cy:
                first = n * ROWS + (0 if cy == 1 else 8)
                corner_tiles[q - 7] = received[first : first + 8]
            copies.append(
                pltpu.make_async_copy(
                    faces.at[end, n, rows], out_hbm.at[q, plane, rows], face_sems.at[end, n]
                )
            )
            copies[-1].start()
    row_index = lax.broadcasted_iota(jnp.int32, (8, LENGTH), 0)
    sides = ((Y_UP, y_up, tiles_up, 0), (Y_DOWN, y_down, tiles_down, 8))
    for side, (group, received, local, begin) in enumerate(sides):
        row = 0 if side == 0 else 7
        for n, q in enumerate(group):
            cx = VELOCITIES[q][0]
            low, high = (1 if cx == 1 else 0), (PLANES - 1 if cx == -1 else PLANES)
            for p in range(low, high):
                tiles[side, n, p] = jnp.where(
                    row_index == row, received[n, p : p + 1, :], local[n, p]
                )
            planes = pl.ds(low, high - low)
            copies.append(
                pltpu.make_async_copy(
                    tiles.at[side, n, planes],
                    out_hbm.at[q, planes, pl.ds(begin, 8)],
                    tile_sems.at[side, n],
                )
            )
            copies[-1].start()
    own_ref[...] = own_a[...] + own_b[...]
    gather_cand(cand, source, 3 * ROWS, 0.0, 0.0)
    for c in range(start, BLOCKS):
        acc[c - start] = acc_in[c]
    codes.wait()
    pair_tiles(0, start, BLOCKS, codes_ref, cand, own_ref, wide_ref, acc, start, listed)
    own_sums(0, start, acc_in, 0, own_ref)
    own_sums(start, BLOCKS, acc, start, own_ref)
    for copy in copies:
        copy.wait()


def pair_cost(tiles):
    return pl.CostEstimate(
        flops=1000000 * tiles, bytes_accessed=1000000, transcendentals=50000 * tiles
    )


BEADS = f32(3, BLOCKS, LANES)
WIDE = f32(BLOCKS, 4, LANES, LANES)
SUMS = f32(BLOCKS, 3, LANES, LANES)
CAND = VMEM((4, BLOCKS, LANES), jnp.float32)
LISTED = [
    pltpu.SMEM((BLOCKS * SHELL + 8,), jnp.int32),
    pltpu.SMEM((SHELL, BLOCKS), jnp.int32),
    pltpu.SemaphoreType.DMA,
]


def pair_a(stop, codes, own, flow):
    return pl.pallas_call(
        functools.partial(pair_a_kernel, stop),
        out_shape=(BEADS, WIDE, f32(3, LENGTH, NODES), SUMS),
        in_specs=[UNREAD] + [WHOLE] * 2,
        out_specs=(WHOLE,) * 4,
        scratch_shapes=[CAND, *LISTED],
        compiler_params=params(20),
        cost_estimate=pair_cost(2 * stop),
        name="pair_a",
    )(codes, own, flow)


def pair_b(stop, codes, own, following, wide, sums, field):
    return pl.pallas_call(
        functools.partial(pair_b_kernel, stop),
        out_shape=(BEADS, BEADS, SUMS, f32(3, NODES, LENGTH)),
        in_specs=[UNREAD] + [WHOLE] * 5,
        out_specs=(WHOLE,) * 4,
        scratch_shapes=[CAND, *LISTED],
        compiler_params=params(20),
        cost_estimate=pair_cost(40),
        name="pair_b",
    )(codes, own, following, wide, sums, field)


def pair_c(codes, side, wide, sums, after):
    return pl.pallas_call(
        pair_c_kernel,
        out_shape=(BEADS, SUMS),
        in_specs=[UNREAD] + [WHOLE] * 3 + [UNREAD],
        out_specs=(WHOLE,) * 2,
        scratch_shapes=[CAND, *LISTED],
        compiler_params=params(20),
        cost_estimate=pair_cost(40),
        name="pair_c",
    )(codes, side, wide, sums, after)


def last(start, out, codes, *operands):
    return pl.pallas_call(
        functools.partial(last_kernel, start),
        out_shape=(f32(Q, PLANES, ROWS, LENGTH), BEADS, f32(4, 8, LENGTH)),
        in_specs=[FAR, UNREAD] + [WHOLE] * 5 + [UNREAD] + [WHOLE] * 6,
        out_specs=(FAR, WHOLE, WHOLE),
        scratch_shapes=[
            CAND,
            *LISTED,
            VMEM((BLOCKS - start, 3, LANES, LANES), jnp.float32),
            VMEM((2, 5, PLANES, 8, LENGTH), jnp.float32),
            VMEM((2, 5, ROWS, LENGTH), jnp.float32),
            pltpu.SemaphoreType.DMA((2, 5)),
            pltpu.SemaphoreType.DMA((2, 5)),
        ],
        input_output_aliases={0: 0},
        compiler_params=params(20),
        cost_estimate=pair_cost(4 * (BLOCKS - start)),
        name="last",
    )(out, codes, *operands)


def hat(steps, fraction):
    return jnp.where(steps == 0.0, 1.0 - fraction, jnp.where(steps == 1.0, fraction, 0.0))


def node_first(k):
    value = jnp.where(k < NODES, lax.shift_right_logical(k, 4), PLANES)
    value = jnp.where(k < NODES + ROWS, value, k - (NODES + ROWS))
    value = jnp.where(k < NODES + ROWS + PLANES, value, PLANES)
    return jnp.where(k < NODES + ROWS + PLANES + 1, value, -8).astype(jnp.float32)


def node_second(k):
    value = jnp.where(k < NODES + ROWS, k & 15, ROWS)
    return jnp.where(k < NODES + ROWS + PLANES + 1, value, -8).astype(jnp.float32)


def halves(value):
    high = value.astype(jnp.bfloat16)
    low = (value - high.astype(jnp.float32)).astype(jnp.bfloat16)
    return high, low


def product(left, right, dims):
    left_high, left_low = left
    right_high, right_low = right
    dot = functools.partial(
        lax.dot_general, dimension_numbers=(dims, ((), ())), preferred_element_type=jnp.float32
    )
    return dot(left_high, right_high) + (dot(left_low, right_high) + dot(left_high, right_low))


DEEP = 48


def friction_kernel(
    bead_ref,
    turned_ref,
    from_next,
    from_side,
    corner_ref,
    drag_ref,
    field_ref,
    ghost_x,
    ghost_y,
    ghost_corner_ref,
    flow_high,
    flow_low,
    total_ref,
):
    extra = WINDOW - NODES
    k_row = lax.broadcasted_iota(jnp.int32, (WINDOW, 1), 0)
    first_row, second_row = node_first(k_row), node_second(k_row)
    depth = lax.broadcasted_iota(jnp.int32, (DEEP, 1), 0).astype(jnp.float32)
    padding = jnp.zeros((extra - ROWS - PLANES - 1, LANES), jnp.float32)
    total_ref[...] = jnp.zeros_like(total_ref)
    for d in range(3):
        for j in range(LENGTH // LANES):
            lanes = slice(j * LANES, (j + 1) * LANES)
            beside = jnp.concatenate(
                [
                    from_next[d * ROWS : (d + 1) * ROWS, lanes],
                    from_side[d * PLANES : (d + 1) * PLANES, lanes],
                    corner_ref[d : d + 1, lanes],
                    padding,
                ],
                axis=0,
            ).T
            high, low = halves(turned_ref[d, lanes, :])
            high_beside, low_beside = halves(beside)
            flow_high[d, lanes, 0:NODES] = high
            flow_low[d, lanes, 0:NODES] = low
            flow_high[d, lanes, NODES:WINDOW] = high_beside
            flow_low[d, lanes, NODES:WINDOW] = low_beside
        flow_high[d, LENGTH : LENGTH + 16, :] = flow_high[d, 0:16, :]
        flow_low[d, LENGTH : LENGTH + 16, :] = flow_low[d, 0:16, :]

    for c in range(BLOCKS):
        span = slice(c * SPAN, c * SPAN + DEEP)
        rows = [bead_ref[k, c : c + 1] for k in range(10)]
        weight = halves(
            hat(first_row - rows[0], rows[3]) * hat(second_row - rows[1], rows[4])
        )
        along = hat(depth - rows[2], rows[5])
        nodes = tuple(
            jnp.concatenate([part[d, span, :] for d in range(3)], axis=0)
            for part in (flow_high, flow_low)
        )
        fluid = product(nodes, weight, ((1,), (0,)))
        pushes = []
        for d in range(3):
            here = jnp.sum(fluid[d * DEEP : (d + 1) * DEEP] * along, axis=0, keepdims=True)
            drag = friction_rate * (here - rows[6 + d]) * rows[9]
            drag_ref[d, c : c + 1, :] = drag
            pushes.append(along * -drag)
        spread = product(halves(jnp.concatenate(pushes, axis=0)), weight, ((1,), (1,)))
        for d in range(3):
            total_ref[d, span, 0:WINDOW] = (
                total_ref[d, span, 0:WINDOW] + spread[d * DEEP : (d + 1) * DEEP]
            )
    ghost_corner_ref[...] = jnp.zeros_like(ghost_corner_ref)
    for d in range(3):
        total_ref[d, 0:16, :] = total_ref[d, 0:16, :] + total_ref[d, LENGTH : LENGTH + 16, :]
        field_ref[d] = total_ref[d, 0:LENGTH, 0:NODES]
        for j in range(LENGTH // LANES):
            lanes = slice(j * LANES, (j + 1) * LANES)
            beside = total_ref[d, lanes, NODES : NODES + LANES].T
            ghost_x[d * ROWS : (d + 1) * ROWS, lanes] = beside[0:ROWS]
            ghost_y[d * PLANES : (d + 1) * PLANES, lanes] = beside[ROWS : ROWS + PLANES]
            ghost_corner_ref[d : d + 1, lanes] = beside[ROWS + PLANES : ROWS + PLANES + 1]


def friction(beads, turned, following, side, corner):
    return pl.pallas_call(
        friction_kernel,
        out_shape=(
            f32(3, BLOCKS, LANES),
            f32(3, LENGTH, NODES),
            f32(3 * ROWS, LENGTH),
            f32(3 * PLANES, LENGTH),
            f32(8, LENGTH),
        ),
        in_specs=[WHOLE] * 5,
        out_specs=(WHOLE,) * 5,
        scratch_shapes=[
            VMEM((3, LENGTH + 16, WINDOW), jnp.bfloat16),
            VMEM((3, LENGTH + 16, WINDOW), jnp.bfloat16),
            VMEM((3, LENGTH + 16, 2 * LANES), jnp.float32),
        ],
        compiler_params=params(24),
        cost_estimate=pl.CostEstimate(flops=60000000, bytes_accessed=3000000, transcendentals=0),
        name="friction",
    )(beads, turned, following, side, corner)


def relaxed_of(p, wanted, pop, field_ref, ghost_x, ghost_y, corner_ref):
    row_index = lax.broadcasted_iota(jnp.int32, (ROWS, LENGTH), 0)
    rho, momentum = moments_of([pop[q, p] for q in range(Q)])
    inverse = 1.0 / rho
    velocity = []
    for d in range(3):
        force = field_ref[d, p * ROWS : (p + 1) * ROWS]
        edge = ghost_y[d * PLANES + p : d * PLANES + p + 1]
        if p == 0:
            force = force + ghost_x[d * ROWS : (d + 1) * ROWS]
            edge = edge + corner_ref[d : d + 1]
        force = force + jnp.where(row_index == 0, edge, 0.0)
        velocity.append((momentum[d] + relaxation * force) * inverse)
    speed = velocity[0] * velocity[0] + velocity[1] * velocity[1] + velocity[2] * velocity[2]
    base = 1.0 - 1.5 * speed
    weights = (rho * (1.25 / 3.0), rho * (1.25 * FACE), rho * (1.25 * EDGE))
    scaled = [component * 4.5**0.5 for component in velocity]
    odd_weights = [weight * 2.0**0.5 for weight in weights]
    if 0 in wanted:
        yield 0, weights[0] * base - 0.25 * pop[0, p]
    for q in range(1, Q, 2):
        if q not in wanted and q + 1 not in wanted:
            continue
        moving = sum(abs(sign) for sign in VELOCITIES[q])
        projected = None
        for sign, component in zip(VELOCITIES[q], scaled):
            if sign == 0:
                continue
            if projected is None:
                projected = component if sign > 0 else -component
            elif sign > 0:
                projected = projected + component
            else:
                projected = projected - component
        even = weights[moving] * (base + projected * projected)
        odd = odd_weights[moving] * projected
        for which, equilibrium in ((q, even + odd), (q + 1, even - odd)):
            if which not in wanted:
                continue
            relaxed = equilibrium - 0.25 * pop[which, p]
            unused, cy, cz = VELOCITIES[which]
            if cz:
                relaxed = pltpu.roll(relaxed, cz % LENGTH, 1)
            if cy:
                relaxed = pltpu.roll(relaxed, cy % ROWS, 0)
            yield which, relaxed


def faces_kernel(
    pop, field_ref, ghost_x, ghost_y, corner_ref, react_ref, first_ref, second_ref
):
    def write(x_up, x_down):
        for d in range(3):
            x_up[5 * ROWS :, d * LANES : (d + 1) * LANES] = react_ref[d]
        x_up[5 * ROWS :, 3 * LANES :] = jnp.zeros((BLOCKS, LANES), jnp.float32)
        x_down[5 * ROWS :, :] = jnp.zeros((BLOCKS, LENGTH), jnp.float32)
        for p, group, face in ((PLANES - 1, X_UP, x_up), (0, X_DOWN, x_down)):
            for q, relaxed in relaxed_of(p, group, pop, field_ref, ghost_x, ghost_y, corner_ref):
                n = group.index(q)
                face[n * ROWS : (n + 1) * ROWS, :] = relaxed

    @pl.when(is_odd())
    def _():
        write(first_ref, second_ref)

    @pl.when(jnp.logical_not(is_odd()))
    def _():
        write(second_ref, first_ref)


class Faces:
    def __init__(self, first_ref, second_ref, side):
        self.swapped = is_odd() if side == 0 else jnp.logical_not(is_odd())
        self.refs = (first_ref, second_ref)

    def __getitem__(self, index):
        first, second = (ref[index] for ref in self.refs)
        return jnp.where(self.swapped, second, first)


def faces(populations, field, ghost_x, ghost_y, corner, react):
    return pl.pallas_call(
        faces_kernel,
        out_shape=(f32(5 * ROWS + BLOCKS, LENGTH),) * 2,
        in_specs=[WHOLE] * 6,
        out_specs=(WHOLE,) * 2,
        compiler_params=params(24),
        cost_estimate=pl.CostEstimate(flops=2000000, bytes_accessed=2000000, transcendentals=0),
        name="faces",
    )(populations, field, ghost_x, ghost_y, corner, react)


def collide_kernel(
    pop,
    field_ref,
    ghost_x,
    ghost_y,
    corner_ref,
    after_ref,
    out_hbm,
    y_up,
    y_down,
    tiles_up,
    tiles_down,
    out,
    out_sems,
):
    del after_ref

    def store(p):
        return pltpu.make_async_copy(out.at[:, p], out_hbm.at[:, p], out_sems.at[p])

    for p in range(PLANES):
        for q, relaxed in relaxed_of(p, range(Q), pop, field_ref, ghost_x, ghost_y, corner_ref):
            cx, cy, unused = VELOCITIES[q]
            target = (p + cx) % PLANES
            out[q, target] = relaxed
            if cy == 1:
                n = Y_UP.index(q)
                y_up[n, target : target + 1, :] = relaxed[0:1]
                tiles_up[n, target] = relaxed[0:8]
            if cy == -1:
                n = Y_DOWN.index(q)
                y_down[n, target : target + 1, :] = relaxed[ROWS - 1 : ROWS]
                tiles_down[n, target] = relaxed[8:16]
        if 2 <= p:
            store(p - 1).start()
    store(0).start()
    store(PLANES - 1).start()
    for p in range(PLANES):
        store(p).wait()


def collide(populations, field, ghost_x, ghost_y, corner, after):
    return pl.pallas_call(
        collide_kernel,
        out_shape=(
            f32(Q, PLANES, ROWS, LENGTH),
            f32(5, PLANES, LENGTH),
            f32(5, PLANES, LENGTH),
            f32(5, PLANES, 8, LENGTH),
            f32(5, PLANES, 8, LENGTH),
        ),
        in_specs=[WHOLE] * 5 + [UNREAD],
        out_specs=(FAR,) + (WHOLE,) * 4,
        scratch_shapes=[
            VMEM((Q, PLANES, ROWS, LENGTH), jnp.float32),
            pltpu.SemaphoreType.DMA((PLANES,)),
        ],
        compiler_params=params(32),
        cost_estimate=pl.CostEstimate(flops=20000000, bytes_accessed=12000000, transcendentals=0),
        name="collide",
    )(populations, field, ghost_x, ghost_y, corner, after)


def forward_kernel(first_ref, second_ref, react_ref, up_ref, down_ref):
    x_up = Faces(first_ref, second_ref, 0)
    x_down = Faces(first_ref, second_ref, 1)
    up_ref[...] = jnp.zeros_like(up_ref)
    down_ref[...] = jnp.zeros_like(down_ref)
    for d in range(3):
        up_ref[8:, d * LANES : (d + 1) * LANES] = react_ref[d]
    rows = [X_UP.index(7) * ROWS, X_DOWN.index(10) * ROWS]
    up_ref[0:1, :] = x_up[rows[0] : rows[0] + 1, :]
    up_ref[1:2, :] = x_down[rows[1] : rows[1] + 1, :]
    rows = [X_UP.index(9) * ROWS + ROWS - 1, X_DOWN.index(8) * ROWS + ROWS - 1]
    down_ref[0:1, :] = x_up[rows[0] : rows[0] + 1, :]
    down_ref[1:2, :] = x_down[rows[1] : rows[1] + 1, :]


def forward(first, second, react):
    return pl.pallas_call(
        forward_kernel,
        out_shape=(f32(8 + BLOCKS, LENGTH), f32(8, LENGTH)),
        in_specs=[WHOLE] * 3,
        out_specs=(WHOLE,) * 2,
        compiler_params=params(8),
        name="forward",
    )(first, second, react)


def finish_kernel(
    out_in,
    corner_tiles,
    first_ref,
    second_ref,
    from_below,
    from_above,
    own_ref,
    drag_ref,
    out_hbm,
    force_ref,
    tiles,
    sems,
):
    del out_in
    x_up = Faces(first_ref, second_ref, 0)
    row_index = lax.broadcasted_iota(jnp.int32, (8, LENGTH), 0)
    sources = {7: from_below[0:1], 10: from_below[1:2], 9: from_above[0:1], 8: from_above[1:2]}
    copies = []
    for q, source in sources.items():
        cx, cy, unused = VELOCITIES[q]
        tiles[q - 7] = jnp.where(row_index == (0 if cy == 1 else 7), source, corner_tiles[q - 7])
        target = out_hbm.at[q, 0 if cx == 1 else PLANES - 1, pl.ds(0 if cy == 1 else 8, 8)]
        copies.append(pltpu.make_async_copy(tiles.at[q - 7], target, sems.at[q - 7]))
        copies[-1].start()
    for d in range(3):
        lanes = slice(d * LANES, (d + 1) * LANES)
        back = x_up[slice(5 * ROWS, None), lanes] + from_below[8:, lanes]
        force_ref[d] = own_ref[d] + back + drag_ref[d]
    for copy in copies:
        copy.wait()


def finish(out, *operands):
    return pl.pallas_call(
        finish_kernel,
        out_shape=(f32(Q, PLANES, ROWS, LENGTH), f32(3, BLOCKS, LANES)),
        in_specs=[FAR] + [WHOLE] * 7,
        out_specs=(FAR, WHOLE),
        scratch_shapes=[VMEM((4, 8, LENGTH), jnp.float32), pltpu.SemaphoreType.DMA((4,))],
        input_output_aliases={0: 0},
        compiler_params=params(8),
        name="finish",
    )(out, *operands)


CUT = 12


def on_device(n_first, n_second, populations, frac, cell, charge, velocity, count, codes):
    def to(value, steps_first, steps_second):
        pairs = [
            (
                i * n_second + j,
                ((i + steps_first) % n_first) * n_second + (j + steps_second) % n_second,
            )
            for i in range(n_first)
            for j in range(n_second)
        ]
        return lax.ppermute(value, ("gx", "gy"), pairs)

    def swap(value, parity):
        pairs = []
        for i in range(n_first):
            partner = (i + 1 if i % 2 == parity else i - 1) % n_first
            pairs += [(i * n_second + j, partner * n_second + j) for j in range(n_second)]
        return lax.ppermute(value, ("gx", "gy"), pairs)

    count, codes = count.reshape(BLOCKS), codes.T
    own, side, corner, beads, flow = start(count, cell, frac, charge, velocity, populations)
    following, side, corner = to(own, -1, 0), to(side, 0, -1), to(corner, -1, -1)
    own_a, wide, turned, sums = pair_a(CUT, codes, own, flow)
    drag, turned, ghost_x, ghost_y, corner = friction(beads, turned, following, side, corner)
    ghost_x, ghost_y, corner = to(ghost_x, 1, 0), to(ghost_y, 0, 1), to(corner, 1, 1)
    own_b, react, sums, field = pair_b(CUT, codes, own, following, wide, sums, turned)
    first, second = faces(populations, field, ghost_x, ghost_y, corner, react)
    out, y_up, y_down, tiles_up, tiles_down = collide(
        populations, field, ghost_x, ghost_y, corner, first
    )
    first, second = swap(first, 1), swap(second, 0)
    y_up, y_down = to(y_up, 0, 1), to(y_down, 0, -1)
    react, sums = pair_c(codes, side, wide, sums, tiles_up)
    up, down = forward(first, second, react)
    from_below, from_above = to(up, 0, 1), to(down, 0, -1)
    out, total, corner_tiles = last(
        CUT,
        out,
        codes,
        own,
        wide,
        sums,
        own_a,
        own_b,
        up,
        first,
        second,
        y_up,
        y_down,
        tiles_up,
        tiles_down,
    )
    out, force = finish(
        out, corner_tiles, first, second, from_below, from_above, total, drag
    )
    return force, out


def solution(mesh):
    return jax.shard_map(
        functools.partial(on_device, mesh.shape["gx"], mesh.shape["gy"]),
        mesh=mesh,
        in_specs=(
            P(None, "gx", "gy", None),
            P(None, "gx", "gy"),
            P("gx", "gy"),
            P("gx", "gy"),
            P(None, "gx", "gy"),
            P("gx", "gy"),
            P("gx", "gy"),
        ),
        out_specs=(P(None, "gx", "gy"), P(None, "gx", "gy", None)),
        check_vma=False,
    )
```

```python
import functools

import jax
import jax.numpy as jnp
import numpy as np
from jax import lax
from jax.experimental import pallas as pl
from jax.experimental.pallas import tpu as pltpu
from jax.sharding import PartitionSpec as P

VELOCITIES = (
    (0, 0, 0),
    (1, 0, 0),
    (-1, 0, 0),
    (0, 1, 0),
    (0, -1, 0),
    (0, 0, 1),
    (0, 0, -1),
    (1, 1, 0),
    (-1, -1, 0),
    (1, -1, 0),
    (-1, 1, 0),
    (1, 0, 1),
    (-1, 0, -1),
    (1, 0, -1),
    (-1, 0, 1),
    (0, 1, 1),
    (0, -1, -1),
    (0, 1, -1),
    (0, -1, 1),
)
Q = 19
FACE = 1.0 / 18.0
EDGE = 1.0 / 36.0
relaxation = 0.8
friction_rate = 8.0
screening = 0.25
softening = 0.25
gauss_term = 0.28209479177387814

STRETCH = 0.45
ERFCX = (
    0.2538730335007913,
    0.2542496247938967,
    0.22382455836296578,
    0.20419679225971624,
    0.007848770232788184,
    0.247605942768305,
    -0.264920441150418,
    0.07332591039690019,
)

PLANES = 8
ROWS = 16
LENGTH = 512
BLOCKS = 16
LANES = 128
SHELL = 6
SPAN = LENGTH // BLOCKS
NODES = PLANES * ROWS
WINDOW = 160

X_UP = tuple(q for q in range(Q) if VELOCITIES[q][0] == 1)
X_DOWN = tuple(q for q in range(Q) if VELOCITIES[q][0] == -1)
Y_UP = tuple(q for q in range(Q) if VELOCITIES[q][1] == 1)
Y_DOWN = tuple(q for q in range(Q) if VELOCITIES[q][1] == -1)
VMEM = pltpu.VMEM
WHOLE = pl.BlockSpec(memory_space=pltpu.VMEM)
UNREAD = pl.BlockSpec(memory_space=pl.ANY)
FAR = pl.BlockSpec(memory_space=pltpu.HBM)


RUN = 32


def is_late():
    return lax.axis_index("gx") % RUN <= 1


def is_odd(axis="gx"):
    return lax.axis_index(axis) % 2 == 1


def params(mib):
    return pltpu.CompilerParams(vmem_limit_bytes=mib * 1024 * 1024)


def f32(*shape):
    return jax.ShapeDtypeStruct(shape, jnp.float32)


def moments_of(pops):
    rho = pops[0]
    for q in range(1, Q):
        rho = rho + pops[q]
    momentum = []
    for d in range(3):
        total = None
        for q in range(Q):
            sign = VELOCITIES[q][d]
            if sign == 0:
                continue
            if total is None:
                total = pops[q]
            elif sign > 0:
                total = total + pops[q]
            else:
                total = total - pops[q]
        momentum.append(total)
    return rho, momentum


def start_kernel(
    count_hbm,
    cell_hbm,
    frac_hbm,
    charge_hbm,
    velocity_hbm,
    pop_hbm,
    send_x,
    send_y,
    send_corner,
    bead_ref,
    flow_ref,
    count_ref,
    cell_ref,
    frac_ref,
    charge_ref,
    velocity_ref,
    pop,
    bead_sems,
    pop_sems,
):
    copies = [
        pltpu.make_async_copy(source, target, bead_sems.at[n])
        for n, (source, target) in enumerate(
            (
                (count_hbm, count_ref),
                (cell_hbm, cell_ref),
                (frac_hbm, frac_ref),
                (charge_hbm, charge_ref),
                (velocity_hbm, velocity_ref),
            )
        )
    ]
    loads = [
        pltpu.make_async_copy(pop_hbm.at[:, p], pop.at[:, p], pop_sems.at[p]) for p in range(PLANES)
    ]
    for copy in copies + loads:
        copy.start()
    block = lax.broadcasted_iota(jnp.int32, (BLOCKS, LANES), 0)
    lane = lax.broadcasted_iota(jnp.int32, (BLOCKS, LANES), 1)
    counts = jnp.zeros((BLOCKS, LANES), jnp.int32)
    for copy in copies:
        copy.wait()
    for c in range(BLOCKS):
        counts = jnp.where(block == c, count_ref[c], counts)
    live = (lane < counts).astype(jnp.float32)
    cell = cell_ref[...]
    first = lax.shift_right_logical(cell, 13)
    second = lax.shift_right_logical(cell, 9) & 15
    third = cell & 511
    start_first = lax.axis_index("gx") * PLANES
    start_second = lax.axis_index("gy") * ROWS
    start_third = block * SPAN
    x = (start_first + first).astype(jnp.float32) + frac_ref[0]
    y = (start_second + second).astype(jnp.float32) + frac_ref[1]
    z = third.astype(jnp.float32) + frac_ref[2]
    x = x - start_first.astype(jnp.float32)
    y = y - start_second.astype(jnp.float32)
    z = z - start_third.astype(jnp.float32)
    for k, value in enumerate((x, y, z, charge_ref[...] * live)):
        send_x[3 * ROWS :, k * LANES : (k + 1) * LANES] = value
        send_y[3 * PLANES :, k * LANES : (k + 1) * LANES] = value
    drags = (
        first.astype(jnp.float32),
        second.astype(jnp.float32),
        (third - start_third).astype(jnp.float32),
        frac_ref[0],
        frac_ref[1],
        frac_ref[2],
        velocity_ref[0],
        velocity_ref[1],
        velocity_ref[2],
        live,
    )
    for k, value in enumerate(drags):
        bead_ref[k] = value
    send_corner[...] = jnp.zeros_like(send_corner)
    for p in range(PLANES):
        loads[p].wait()
        rho, momentum = moments_of([pop[q, p] for q in range(Q)])
        inverse = 1.0 / rho
        for d in range(3):
            flow = momentum[d] * inverse
            flow_ref[d, p * ROWS : (p + 1) * ROWS, :] = flow
            send_y[d * PLANES + p : d * PLANES + p + 1, :] = flow[0:1]
            if p == 0:
                send_x[d * ROWS : (d + 1) * ROWS, :] = flow
                send_corner[d : d + 1, :] = flow[0:1]


def start(*arrays):
    far = [pltpu.with_memory_space_constraint(array, pltpu.HBM) for array in arrays]
    return pl.pallas_call(
        start_kernel,
        out_shape=(
            f32(3 * ROWS + BLOCKS, LENGTH),
            f32(3 * PLANES + BLOCKS, LENGTH),
            f32(8, LENGTH),
            f32(10, BLOCKS, LANES),
            f32(3, NODES, LENGTH),
        ),
        in_specs=[FAR] * 6,
        out_specs=(WHOLE,) * 5,
        scratch_shapes=[
            pltpu.SMEM((BLOCKS,), jnp.int32),
            VMEM((BLOCKS, LANES), jnp.int32),
            VMEM((3, BLOCKS, LANES), jnp.float32),
            VMEM((BLOCKS, LANES), jnp.float32),
            VMEM((3, BLOCKS, LANES), jnp.float32),
            VMEM((Q, PLANES, ROWS, LENGTH), jnp.float32),
            pltpu.SemaphoreType.DMA((5,)),
            pltpu.SemaphoreType.DMA((PLANES,)),
        ],
        compiler_params=params(20),
        cost_estimate=pl.CostEstimate(flops=4000000, bytes_accessed=6000000, transcendentals=0),
        name="start",
    )(*far)


def radial_of(s):
    r = lax.rsqrt(s)
    rr = s * r
    below = 1.0 + (STRETCH * screening) * rr
    t = pl.reciprocal(below, approx=True)
    t = t * (2.0 - below * t)
    poly = jnp.full_like(t, ERFCX[-1])
    for coefficient in ERFCX[-2::-1]:
        poly = poly * t + coefficient
    decay = jnp.exp2(s * (-screening * screening * 1.4426950408889634))
    return decay * (poly * t * r + gauss_term) * (r * r)


def pair_tiles(kind, start, stop, codes_ref, cand_ref, react_ref, wide_ref, acc, base, listed):
    count = jnp.int32(0)
    for c in range(start, stop):
        for s in range(SHELL):
            code = codes_ref[s, c]
            listed[count] = (code & 15) + BLOCKS * c
            count = count + (lax.shift_right_logical(code, 4) == kind).astype(jnp.int32)

    def tile(i, carry):
        entry = listed[i]
        c = lax.shift_right_logical(entry, 4)
        e = entry & 15
        n = c - base
        steps = e - c
        steps = jnp.where(steps > 1, steps - BLOCKS, steps)
        steps = jnp.where(steps < -1, steps + BLOCKS, steps)
        shift_third = (steps * SPAN).astype(jnp.float32)
        xj, yj, zj, qj = (cand_ref[k, pl.ds(e, 1), :] for k in range(4))
        zj = zj + shift_third
        xj, yj, zj, qj = (jnp.broadcast_to(v, (8, LANES)) for v in (xj, yj, zj, qj))
        j = lax.broadcasted_iota(jnp.int32, (8, LANES), 1)
        j = j - lax.broadcasted_iota(jnp.int32, (8, LANES), 0) + LANES * jnp.abs(steps)
        sums = [jnp.zeros((8, LANES), jnp.float32) for _ in range(3)]
        for g in range(LANES // 8):
            rows = slice(8 * g, 8 * g + 8)
            dx = wide_ref[c, 0, rows] - xj
            dy = wide_ref[c, 1, rows] - yj
            dz = wide_ref[c, 2, rows] - zj
            squares = dx * dx + dy * dy + dz * dz + softening
            strength = wide_ref[c, 3, rows] * qj * radial_of(squares)
            if kind == 0:
                strength = jnp.where(j == 8 * g, 0.0, strength)
            for d, delta in enumerate((dx, dy, dz)):
                force = strength * delta
                acc[n, d, rows] = acc[n, d, rows] + force
                sums[d] = sums[d] + force
        for d in range(3):
            total = jnp.sum(sums[d], axis=0, keepdims=True)
            react_ref[d, pl.ds(e, 1), :] = react_ref[d, pl.ds(e, 1), :] - total
        return carry

    lax.fori_loop(0, count, tile, 0)


def copy_sums(acc_in, acc):
    def block(c, carry):
        acc[c] = acc_in[c]
        return carry

    lax.fori_loop(0, BLOCKS, block, 0)


def own_sums(start, stop, acc, base, own_ref):
    j = lax.broadcasted_iota(jnp.int32, (8, LANES), 1)
    j = j - lax.broadcasted_iota(jnp.int32, (8, LANES), 0)
    for c in range(start, stop):
        for d in range(3):
            own = jnp.zeros((8, LANES), jnp.float32)
            for g in range(LANES // 8):
                column = jnp.sum(acc[c - base, d, 8 * g : 8 * g + 8], axis=1, keepdims=True)
                own = own + jnp.where(j == 8 * g, column, 0.0)
            own = jnp.sum(own, axis=0, keepdims=True)
            own_ref[d, c : c + 1, :] = own_ref[d, c : c + 1, :] + own


def gather_cand(cand, source, start, shift_first, shift_second):
    for k, shift in enumerate((shift_first, shift_second, 0.0, 0.0)):
        cand[k] = source[start:, k * LANES : (k + 1) * LANES] + shift


def pair_a_kernel(
    stop,
    codes_hbm,
    source,
    flow_ref,
    own_ref,
    wide_ref,
    turned_ref,
    acc,
    cand,
    listed,
    codes_ref,
    codes_sem,
):
    codes = pltpu.make_async_copy(codes_hbm, codes_ref, codes_sem)
    codes.start()
    gather_cand(cand, source, 3 * ROWS, 0.0, 0.0)
    for d in range(3):
        for j in range(LENGTH // LANES):
            lanes = slice(j * LANES, (j + 1) * LANES)
            turned_ref[d, lanes, :] = flow_ref[d, :, lanes].T
    columns = [cand[k].T for k in range(4)]
    for c in range(BLOCKS):
        for k in range(4):
            wide_ref[c, k] = jnp.broadcast_to(columns[k][:, c : c + 1], (LANES, LANES))
    own_ref[...] = jnp.zeros_like(own_ref)

    def clear(c, carry):
        acc[c] = jnp.zeros((3, LANES, LANES), jnp.float32)
        return carry

    lax.fori_loop(0, BLOCKS, clear, 0)

    codes.wait()

    @pl.when(jnp.logical_not(is_late()))
    def _():
        pair_tiles(0, 0, stop, codes_ref, cand, own_ref, wide_ref, acc, 0, listed)


def pair_b_kernel(
    stop,
    codes_hbm,
    own_source,
    source,
    wide_ref,
    acc_in,
    turned_ref,
    own_ref,
    react_ref,
    acc,
    field_ref,
    cand,
    listed,
    codes_ref,
    codes_sem,
):
    codes = pltpu.make_async_copy(codes_hbm, codes_ref, codes_sem)
    codes.start()
    for d in range(3):
        for j in range(LENGTH // LANES):
            lanes = slice(j * LANES, (j + 1) * LANES)
            field_ref[d, :, lanes] = turned_ref[d, lanes, :].T
    own_ref[...] = jnp.zeros_like(own_ref)
    react_ref[...] = jnp.zeros_like(react_ref)
    copy_sums(acc_in, acc)
    gather_cand(cand, source, 3 * ROWS, float(PLANES), 0.0)
    codes.wait()
    pair_tiles(1, 0, BLOCKS, codes_ref, cand, react_ref, wide_ref, acc, 0, listed)

    @pl.when(is_late())
    def _():
        gather_cand(cand, own_source, 3 * ROWS, 0.0, 0.0)
        pair_tiles(0, 0, stop, codes_ref, cand, own_ref, wide_ref, acc, 0, listed)


def pair_c_kernel(
    codes_hbm,
    source,
    wide_ref,
    acc_in,
    after_ref,
    react_ref,
    acc,
    cand,
    listed,
    codes_ref,
    codes_sem,
):
    del after_ref
    codes = pltpu.make_async_copy(codes_hbm, codes_ref, codes_sem)
    codes.start()
    gather_cand(cand, source, 3 * PLANES, 0.0, float(ROWS))
    react_ref[...] = jnp.zeros_like(react_ref)
    copy_sums(acc_in, acc)
    codes.wait()
    pair_tiles(2, 0, BLOCKS, codes_ref, cand, react_ref, wide_ref, acc, 0, listed)


def last_kernel(
    start,
    out_in,
    codes_hbm,
    source,
    wide_ref,
    acc_in,
    own_a,
    own_b,
    after_ref,
    first_ref,
    second_ref,
    y_first,
    y_second,
    tiles_up,
    tiles_down,
    out_hbm,
    own_ref,
    corner_tiles,
    cand,
    listed,
    codes_ref,
    codes_sem,
    acc,
    tiles,
    faces,
    tile_sems,
    face_sems,
):
    del out_in, after_ref
    x_up = Faces(first_ref, second_ref, 0)
    x_down = Faces(first_ref, second_ref, 1)
    y_up = Faces(y_first, y_second, 0, "gy")
    y_down = Faces(y_first, y_second, 1, "gy")
    codes = pltpu.make_async_copy(codes_hbm, codes_ref, codes_sem)
    codes.start()
    copies = []
    for end, (group, received, plane) in enumerate(((X_UP, x_up, 0), (X_DOWN, x_down, PLANES - 1))):
        for n, q in enumerate(group):
            cy = VELOCITIES[q][1]
            faces[end, n] = received[n * ROWS : (n + 1) * ROWS]
            rows = pl.ds((0, 8, 0)[cy], ROWS if cy == 0 else 8)
            if cy:
                first = n * ROWS + (0 if cy == 1 else 8)
                corner_tiles[q - 7] = received[first : first + 8]
            copies.append(
                pltpu.make_async_copy(
                    faces.at[end, n, rows], out_hbm.at[q, plane, rows], face_sems.at[end, n]
                )
            )
            copies[-1].start()
    row_index = lax.broadcasted_iota(jnp.int32, (8, LENGTH), 0)
    sides = ((Y_UP, y_up, tiles_up, 0), (Y_DOWN, y_down, tiles_down, 8))
    for side, (group, received, local, begin) in enumerate(sides):
        row = 0 if side == 0 else 7
        for n, q in enumerate(group):
            cx = VELOCITIES[q][0]
            low, high = (1 if cx == 1 else 0), (PLANES - 1 if cx == -1 else PLANES)
            for p in range(low, high):
                tiles[side, n, p] = jnp.where(
                    row_index == row, received[n, p : p + 1, :], local[n, p]
                )
            planes = pl.ds(low, high - low)
            copies.append(
                pltpu.make_async_copy(
                    tiles.at[side, n, planes],
                    out_hbm.at[q, planes, pl.ds(begin, 8)],
                    tile_sems.at[side, n],
                )
            )
            copies[-1].start()
    own_ref[...] = own_a[...] + own_b[...]
    gather_cand(cand, source, 3 * ROWS, 0.0, 0.0)
    for c in range(start, BLOCKS):
        acc[c - start] = acc_in[c]
    codes.wait()
    pair_tiles(0, start, BLOCKS, codes_ref, cand, own_ref, wide_ref, acc, start, listed)
    own_sums(0, start, acc_in, 0, own_ref)
    own_sums(start, BLOCKS, acc, start, own_ref)
    for copy in copies:
        copy.wait()


def pair_cost(tiles):
    return pl.CostEstimate(
        flops=1000000 * tiles, bytes_accessed=1000000, transcendentals=50000 * tiles
    )


BEADS = f32(3, BLOCKS, LANES)
WIDE = f32(BLOCKS, 4, LANES, LANES)
SUMS = f32(BLOCKS, 3, LANES, LANES)
CAND = VMEM((4, BLOCKS, LANES), jnp.float32)
LISTED = [
    pltpu.SMEM((BLOCKS * SHELL + 8,), jnp.int32),
    pltpu.SMEM((SHELL, BLOCKS), jnp.int32),
    pltpu.SemaphoreType.DMA,
]


def pair_a(stop, codes, own, flow):
    return pl.pallas_call(
        functools.partial(pair_a_kernel, stop),
        out_shape=(BEADS, WIDE, f32(3, LENGTH, NODES), SUMS),
        in_specs=[UNREAD] + [WHOLE] * 2,
        out_specs=(WHOLE,) * 4,
        scratch_shapes=[CAND, *LISTED],
        compiler_params=params(20),
        cost_estimate=pair_cost(2 * stop),
        name="pair_a",
    )(codes, own, flow)


def pair_b(stop, codes, own, following, wide, sums, field):
    return pl.pallas_call(
        functools.partial(pair_b_kernel, stop),
        out_shape=(BEADS, BEADS, SUMS, f32(3, NODES, LENGTH)),
        in_specs=[UNREAD] + [WHOLE] * 5,
        out_specs=(WHOLE,) * 4,
        scratch_shapes=[CAND, *LISTED],
        compiler_params=params(20),
        cost_estimate=pair_cost(40),
        name="pair_b",
    )(codes, own, following, wide, sums, field)


def pair_c(codes, side, wide, sums, after):
    return pl.pallas_call(
        pair_c_kernel,
        out_shape=(BEADS, SUMS),
        in_specs=[UNREAD] + [WHOLE] * 3 + [UNREAD],
        out_specs=(WHOLE,) * 2,
        scratch_shapes=[CAND, *LISTED],
        compiler_params=params(20),
        cost_estimate=pair_cost(40),
        name="pair_c",
    )(codes, side, wide, sums, after)


def last(start, out, codes, *operands):
    return pl.pallas_call(
        functools.partial(last_kernel, start),
        out_shape=(f32(Q, PLANES, ROWS, LENGTH), BEADS, f32(4, 8, LENGTH)),
        in_specs=[FAR, UNREAD] + [WHOLE] * 5 + [UNREAD] + [WHOLE] * 6,
        out_specs=(FAR, WHOLE, WHOLE),
        scratch_shapes=[
            CAND,
            *LISTED,
            VMEM((BLOCKS - start, 3, LANES, LANES), jnp.float32),
            VMEM((2, 5, PLANES, 8, LENGTH), jnp.float32),
            VMEM((2, 5, ROWS, LENGTH), jnp.float32),
            pltpu.SemaphoreType.DMA((2, 5)),
            pltpu.SemaphoreType.DMA((2, 5)),
        ],
        input_output_aliases={0: 0},
        compiler_params=params(20),
        cost_estimate=pair_cost(4 * (BLOCKS - start)),
        name="last",
    )(out, codes, *operands)


def hat(steps, fraction):
    return jnp.where(steps == 0.0, 1.0 - fraction, jnp.where(steps == 1.0, fraction, 0.0))


def node_first(k):
    value = jnp.where(k < NODES, lax.shift_right_logical(k, 4), PLANES)
    value = jnp.where(k < NODES + ROWS, value, k - (NODES + ROWS))
    value = jnp.where(k < NODES + ROWS + PLANES, value, PLANES)
    return jnp.where(k < NODES + ROWS + PLANES + 1, value, -8).astype(jnp.float32)


def node_second(k):
    value = jnp.where(k < NODES + ROWS, k & 15, ROWS)
    return jnp.where(k < NODES + ROWS + PLANES + 1, value, -8).astype(jnp.float32)


def halves(value):
    high = value.astype(jnp.bfloat16)
    low = (value - high.astype(jnp.float32)).astype(jnp.bfloat16)
    return high, low


def product(left, right, dims):
    left_high, left_low = left
    right_high, right_low = right
    dot = functools.partial(
        lax.dot_general, dimension_numbers=(dims, ((), ())), preferred_element_type=jnp.float32
    )
    return dot(left_high, right_high) + (dot(left_low, right_high) + dot(left_high, right_low))


DEEP = 48


def friction_kernel(
    bead_ref,
    turned_ref,
    from_next,
    from_side,
    corner_ref,
    drag_ref,
    field_ref,
    ghost_x,
    ghost_y,
    ghost_corner_ref,
    flow_high,
    flow_low,
    total_ref,
):
    extra = WINDOW - NODES
    k_row = lax.broadcasted_iota(jnp.int32, (WINDOW, 1), 0)
    first_row, second_row = node_first(k_row), node_second(k_row)
    depth = lax.broadcasted_iota(jnp.int32, (DEEP, 1), 0).astype(jnp.float32)
    padding = jnp.zeros((extra - ROWS - PLANES - 1, LANES), jnp.float32)
    total_ref[...] = jnp.zeros_like(total_ref)
    for d in range(3):
        for j in range(LENGTH // LANES):
            lanes = slice(j * LANES, (j + 1) * LANES)
            beside = jnp.concatenate(
                [
                    from_next[d * ROWS : (d + 1) * ROWS, lanes],
                    from_side[d * PLANES : (d + 1) * PLANES, lanes],
                    corner_ref[d : d + 1, lanes],
                    padding,
                ],
                axis=0,
            ).T
            high, low = halves(turned_ref[d, lanes, :])
            high_beside, low_beside = halves(beside)
            flow_high[d, lanes, 0:NODES] = high
            flow_low[d, lanes, 0:NODES] = low
            flow_high[d, lanes, NODES:WINDOW] = high_beside
            flow_low[d, lanes, NODES:WINDOW] = low_beside
        flow_high[d, LENGTH : LENGTH + 16, :] = flow_high[d, 0:16, :]
        flow_low[d, LENGTH : LENGTH + 16, :] = flow_low[d, 0:16, :]

    for c in range(BLOCKS):
        span = slice(c * SPAN, c * SPAN + DEEP)
        rows = [bead_ref[k, c : c + 1] for k in range(10)]
        weight = halves(
            hat(first_row - rows[0], rows[3]) * hat(second_row - rows[1], rows[4])
        )
        along = hat(depth - rows[2], rows[5])
        nodes = tuple(
            jnp.concatenate([part[d, span, :] for d in range(3)], axis=0)
            for part in (flow_high, flow_low)
        )
        fluid = product(nodes, weight, ((1,), (0,)))
        pushes = []
        for d in range(3):
            here = jnp.sum(fluid[d * DEEP : (d + 1) * DEEP] * along, axis=0, keepdims=True)
            drag = friction_rate * (here - rows[6 + d]) * rows[9]
            drag_ref[d, c : c + 1, :] = drag
            pushes.append(along * -drag)
        spread = product(halves(jnp.concatenate(pushes, axis=0)), weight, ((1,), (1,)))
        for d in range(3):
            total_ref[d, span, 0:WINDOW] = (
                total_ref[d, span, 0:WINDOW] + spread[d * DEEP : (d + 1) * DEEP]
            )
    ghost_corner_ref[...] = jnp.zeros_like(ghost_corner_ref)
    for d in range(3):
        total_ref[d, 0:16, :] = total_ref[d, 0:16, :] + total_ref[d, LENGTH : LENGTH + 16, :]
        field_ref[d] = total_ref[d, 0:LENGTH, 0:NODES]
        for j in range(LENGTH // LANES):
            lanes = slice(j * LANES, (j + 1) * LANES)
            beside = total_ref[d, lanes, NODES : NODES + LANES].T
            ghost_x[d * ROWS : (d + 1) * ROWS, lanes] = beside[0:ROWS]
            ghost_y[d * PLANES : (d + 1) * PLANES, lanes] = beside[ROWS : ROWS + PLANES]
            ghost_corner_ref[d : d + 1, lanes] = beside[ROWS + PLANES : ROWS + PLANES + 1]


def friction(beads, turned, following, side, corner):
    return pl.pallas_call(
        friction_kernel,
        out_shape=(
            f32(3, BLOCKS, LANES),
            f32(3, LENGTH, NODES),
            f32(3 * ROWS, LENGTH),
            f32(3 * PLANES, LENGTH),
            f32(8, LENGTH),
        ),
        in_specs=[WHOLE] * 5,
        out_specs=(WHOLE,) * 5,
        scratch_shapes=[
            VMEM((3, LENGTH + 16, WINDOW), jnp.bfloat16),
            VMEM((3, LENGTH + 16, WINDOW), jnp.bfloat16),
            VMEM((3, LENGTH + 16, 2 * LANES), jnp.float32),
        ],
        compiler_params=params(24),
        cost_estimate=pl.CostEstimate(flops=60000000, bytes_accessed=3000000, transcendentals=0),
        name="friction",
    )(beads, turned, following, side, corner)


def relaxed_of(p, wanted, pop, field_ref, ghost_x, ghost_y, corner_ref):
    row_index = lax.broadcasted_iota(jnp.int32, (ROWS, LENGTH), 0)
    rho, momentum = moments_of([pop[q, p] for q in range(Q)])
    inverse = 1.0 / rho
    velocity = []
    for d in range(3):
        force = field_ref[d, p * ROWS : (p + 1) * ROWS]
        edge = ghost_y[d * PLANES + p : d * PLANES + p + 1]
        if p == 0:
            force = force + ghost_x[d * ROWS : (d + 1) * ROWS]
            edge = edge + corner_ref[d : d + 1]
        force = force + jnp.where(row_index == 0, edge, 0.0)
        velocity.append((momentum[d] + relaxation * force) * inverse)
    speed = velocity[0] * velocity[0] + velocity[1] * velocity[1] + velocity[2] * velocity[2]
    base = 1.0 - 1.5 * speed
    weights = (rho * (1.25 / 3.0), rho * (1.25 * FACE), rho * (1.25 * EDGE))
    scaled = [component * 4.5**0.5 for component in velocity]
    odd_weights = [weight * 2.0**0.5 for weight in weights]
    if 0 in wanted:
        yield 0, weights[0] * base - 0.25 * pop[0, p]
    for q in range(1, Q, 2):
        if q not in wanted and q + 1 not in wanted:
            continue
        moving = sum(abs(sign) for sign in VELOCITIES[q])
        projected = None
        for sign, component in zip(VELOCITIES[q], scaled):
            if sign == 0:
                continue
            if projected is None:
                projected = component if sign > 0 else -component
            elif sign > 0:
                projected = projected + component
            else:
                projected = projected - component
        even = weights[moving] * (base + projected * projected)
        odd = odd_weights[moving] * projected
        for which, equilibrium in ((q, even + odd), (q + 1, even - odd)):
            if which not in wanted:
                continue
            relaxed = equilibrium - 0.25 * pop[which, p]
            unused, cy, cz = VELOCITIES[which]
            if cz:
                relaxed = pltpu.roll(relaxed, cz % LENGTH, 1)
            if cy:
                relaxed = pltpu.roll(relaxed, cy % ROWS, 0)
            yield which, relaxed


def faces_kernel(
    pop, field_ref, ghost_x, ghost_y, corner_ref, react_ref, first_ref, second_ref
):
    def write(x_up, x_down):
        for d in range(3):
            x_up[5 * ROWS :, d * LANES : (d + 1) * LANES] = react_ref[d]
        x_up[5 * ROWS :, 3 * LANES :] = jnp.zeros((BLOCKS, LANES), jnp.float32)
        x_down[5 * ROWS :, :] = jnp.zeros((BLOCKS, LENGTH), jnp.float32)
        for p, group, face in ((PLANES - 1, X_UP, x_up), (0, X_DOWN, x_down)):
            for q, relaxed in relaxed_of(p, group, pop, field_ref, ghost_x, ghost_y, corner_ref):
                n = group.index(q)
                face[n * ROWS : (n + 1) * ROWS, :] = relaxed

    @pl.when(is_odd())
    def _():
        write(first_ref, second_ref)

    @pl.when(jnp.logical_not(is_odd()))
    def _():
        write(second_ref, first_ref)


class Faces:
    def __init__(self, first_ref, second_ref, side, axis="gx"):
        self.swapped = is_odd(axis) if side == 0 else jnp.logical_not(is_odd(axis))
        self.refs = (first_ref, second_ref)

    def __getitem__(self, index):
        first, second = (ref[index] for ref in self.refs)
        return jnp.where(self.swapped, second, first)


def faces(populations, field, ghost_x, ghost_y, corner, react):
    return pl.pallas_call(
        faces_kernel,
        out_shape=(f32(5 * ROWS + BLOCKS, LENGTH),) * 2,
        in_specs=[WHOLE] * 6,
        out_specs=(WHOLE,) * 2,
        compiler_params=params(24),
        cost_estimate=pl.CostEstimate(flops=2000000, bytes_accessed=2000000, transcendentals=0),
        name="faces",
    )(populations, field, ghost_x, ghost_y, corner, react)


def collide_kernel(
    pop,
    field_ref,
    ghost_x,
    ghost_y,
    corner_ref,
    after_ref,
    out_hbm,
    y_first,
    y_second,
    tiles_up,
    tiles_down,
    out,
    out_sems,
    y_up,
    y_down,
):
    del after_ref

    def store(p):
        return pltpu.make_async_copy(out.at[:, p], out_hbm.at[:, p], out_sems.at[p])

    for p in range(PLANES):
        for q, relaxed in relaxed_of(p, range(Q), pop, field_ref, ghost_x, ghost_y, corner_ref):
            cx, cy, unused = VELOCITIES[q]
            target = (p + cx) % PLANES
            out[q, target] = relaxed
            if cy == 1:
                n = Y_UP.index(q)
                y_up[n, target : target + 1, :] = relaxed[0:1]
                tiles_up[n, target] = relaxed[0:8]
            if cy == -1:
                n = Y_DOWN.index(q)
                y_down[n, target : target + 1, :] = relaxed[ROWS - 1 : ROWS]
                tiles_down[n, target] = relaxed[8:16]
        if 2 <= p:
            store(p - 1).start()
    store(0).start()
    store(PLANES - 1).start()
    odd = is_odd("gy")
    y_first[...] = jnp.where(odd, y_up[...], y_down[...])
    y_second[...] = jnp.where(odd, y_down[...], y_up[...])
    for p in range(PLANES):
        store(p).wait()


def collide(populations, field, ghost_x, ghost_y, corner, after):
    return pl.pallas_call(
        collide_kernel,
        out_shape=(
            f32(Q, PLANES, ROWS, LENGTH),
            f32(5, PLANES, LENGTH),
            f32(5, PLANES, LENGTH),
            f32(5, PLANES, 8, LENGTH),
            f32(5, PLANES, 8, LENGTH),
        ),
        in_specs=[WHOLE] * 5 + [UNREAD],
        out_specs=(FAR,) + (WHOLE,) * 4,
        scratch_shapes=[
            VMEM((Q, PLANES, ROWS, LENGTH), jnp.float32),
            pltpu.SemaphoreType.DMA((PLANES,)),
            VMEM((5, PLANES, LENGTH), jnp.float32),
            VMEM((5, PLANES, LENGTH), jnp.float32),
        ],
        compiler_params=params(32),
        cost_estimate=pl.CostEstimate(flops=20000000, bytes_accessed=12000000, transcendentals=0),
        name="collide",
    )(populations, field, ghost_x, ghost_y, corner, after)


def forward_kernel(first_ref, second_ref, react_ref, one_ref, two_ref, up_ref, down_ref):
    x_up = Faces(first_ref, second_ref, 0)
    x_down = Faces(first_ref, second_ref, 1)
    up_ref[...] = jnp.zeros_like(up_ref)
    down_ref[...] = jnp.zeros_like(down_ref)
    for d in range(3):
        up_ref[8:, d * LANES : (d + 1) * LANES] = react_ref[d]
    rows = [X_UP.index(7) * ROWS, X_DOWN.index(10) * ROWS]
    up_ref[0:1, :] = x_up[rows[0] : rows[0] + 1, :]
    up_ref[1:2, :] = x_down[rows[1] : rows[1] + 1, :]
    rows = [X_UP.index(9) * ROWS + ROWS - 1, X_DOWN.index(8) * ROWS + ROWS - 1]
    down_ref[0:1, :] = x_up[rows[0] : rows[0] + 1, :]
    down_ref[1:2, :] = x_down[rows[1] : rows[1] + 1, :]
    odd = is_odd("gy")
    one_ref[...] = jnp.where(odd, up_ref[...], down_ref[...])
    two_ref[...] = jnp.where(odd, down_ref[...], up_ref[...])


def forward(first, second, react):
    return pl.pallas_call(
        forward_kernel,
        out_shape=(f32(8 + BLOCKS, LENGTH),) * 2,
        in_specs=[WHOLE] * 3,
        out_specs=(WHOLE,) * 2,
        scratch_shapes=[VMEM((8 + BLOCKS, LENGTH), jnp.float32)] * 2,
        compiler_params=params(8),
        name="forward",
    )(first, second, react)


def finish_kernel(
    out_in,
    corner_tiles,
    first_ref,
    second_ref,
    one_ref,
    two_ref,
    own_ref,
    drag_ref,
    out_hbm,
    force_ref,
    tiles,
    sems,
):
    del out_in
    x_up = Faces(first_ref, second_ref, 0)
    from_below = Faces(one_ref, two_ref, 0, "gy")
    from_above = Faces(one_ref, two_ref, 1, "gy")
    row_index = lax.broadcasted_iota(jnp.int32, (8, LENGTH), 0)
    sources = {7: from_below[0:1], 10: from_below[1:2], 9: from_above[0:1], 8: from_above[1:2]}
    copies = []
    for q, source in sources.items():
        cx, cy, unused = VELOCITIES[q]
        tiles[q - 7] = jnp.where(row_index == (0 if cy == 1 else 7), source, corner_tiles[q - 7])
        target = out_hbm.at[q, 0 if cx == 1 else PLANES - 1, pl.ds(0 if cy == 1 else 8, 8)]
        copies.append(pltpu.make_async_copy(tiles.at[q - 7], target, sems.at[q - 7]))
        copies[-1].start()
    for d in range(3):
        lanes = slice(d * LANES, (d + 1) * LANES)
        back = x_up[slice(5 * ROWS, None), lanes] + from_below[slice(8, None), lanes]
        force_ref[d] = own_ref[d] + back + drag_ref[d]
    for copy in copies:
        copy.wait()


def finish(out, *operands):
    return pl.pallas_call(
        finish_kernel,
        out_shape=(f32(Q, PLANES, ROWS, LENGTH), f32(3, BLOCKS, LANES)),
        in_specs=[FAR] + [WHOLE] * 7,
        out_specs=(FAR, WHOLE),
        scratch_shapes=[VMEM((4, 8, LENGTH), jnp.float32), pltpu.SemaphoreType.DMA((4,))],
        input_output_aliases={0: 0},
        compiler_params=params(8),
        name="finish",
    )(out, *operands)


CUT = 12


def on_device(n_first, n_second, populations, frac, cell, charge, velocity, count, codes):
    def to(value, steps_first, steps_second):
        pairs = [
            (
                i * n_second + j,
                ((i + steps_first) % n_first) * n_second + (j + steps_second) % n_second,
            )
            for i in range(n_first)
            for j in range(n_second)
        ]
        return lax.ppermute(value, ("gx", "gy"), pairs)

    def swap(value, parity):
        pairs = []
        for i in range(n_first):
            partner = (i + 1 if i % 2 == parity else i - 1) % n_first
            pairs += [(i * n_second + j, partner * n_second + j) for j in range(n_second)]
        return lax.ppermute(value, ("gx", "gy"), pairs)

    def swap_side(value, parity):
        pairs = []
        for j in range(n_second):
            partner = (j + 1 if j % 2 == parity else j - 1) % n_second
            pairs += [(i * n_second + j, i * n_second + partner) for i in range(n_first)]
        return lax.ppermute(value, ("gx", "gy"), pairs)

    count, codes = count.reshape(BLOCKS), codes.T
    own, side, corner, beads, flow = start(count, cell, frac, charge, velocity, populations)
    following, side, corner = to(own, -1, 0), to(side, 0, -1), to(corner, -1, -1)
    own_a, wide, turned, sums = pair_a(CUT, codes, own, flow)
    drag, turned, ghost_x, ghost_y, corner = friction(beads, turned, following, side, corner)
    ghost_x, ghost_y, corner = to(ghost_x, 1, 0), to(ghost_y, 0, 1), to(corner, 1, 1)
    own_b, react, sums, field = pair_b(CUT, codes, own, following, wide, sums, turned)
    first, second = faces(populations, field, ghost_x, ghost_y, corner, react)
    out, y_first, y_second, tiles_up, tiles_down = collide(
        populations, field, ghost_x, ghost_y, corner, first
    )
    first, second = swap(first, 1), swap(second, 0)
    y_first, y_second = swap_side(y_first, 1), swap_side(y_second, 0)
    react, sums = pair_c(codes, side, wide, sums, tiles_up)
    one, two = forward(first, second, react)
    one_back, two_back = swap_side(one, 1), swap_side(two, 0)
    out, total, corner_tiles = last(
        CUT,
        out,
        codes,
        own,
        wide,
        sums,
        own_a,
        own_b,
        one,
        first,
        second,
        y_first,
        y_second,
        tiles_up,
        tiles_down,
    )
    out, force = finish(
        out, corner_tiles, first, second, one_back, two_back, total, drag
    )
    return force, out


def solution(mesh):
    return jax.shard_map(
        functools.partial(on_device, mesh.shape["gx"], mesh.shape["gy"]),
        mesh=mesh,
        in_specs=(
            P(None, "gx", "gy", None),
            P(None, "gx", "gy"),
            P("gx", "gy"),
            P("gx", "gy"),
            P(None, "gx", "gy"),
            P("gx", "gy"),
            P("gx", "gy"),
        ),
        out_specs=(P(None, "gx", "gy"), P(None, "gx", "gy", None)),
        check_vma=False,
    )
```
